512 devices in a mesh: dp: 4 (over x), expert: 8 (over z_lo, core), tensor: 16 (over z_hi, y).
Axes of the slice: x: 4, y: 4, z: 16 (z_hi: 4, z_lo: 4; z = z_hi * 4 + z_lo), core: 2. Of those that a mesh axis runs over, the one named last changes fastest.
Arguments:
- pool: bfloat16 [512, 6144], P(('dp', 'expert'), 'tensor'), may hold values from -24 to 24
- prompt_ids: int32 [256, 24], replicated, may hold values from 0 to 511
- tenant: int32 [32], P(('dp', 'expert')), may hold values from 0 to 255
- lengths: int32 [32], P(('dp', 'expert')), may hold values from 1 to 24
- routes: int32 [768, 2], P(('dp', 'expert')), may hold values from 0 to 7, all different within a row; in each aligned block of 24 rows (0 to 23, 24 to 47, ...) at most 8 rows name the same one
- route_weight: float32 [768, 2], P(('dp', 'expert')), may hold values from 0.1 to 1
- cotangent: bfloat16 [768, 6144], P(('dp', 'expert'), 'tensor'), may hold values from -6 to 6
- norm_gain: bfloat16 [6144], replicated, may hold values from 0.3 to 3
- w_gate: bfloat16 [8, 6144, 8192], P('expert', None, ('dp', 'tensor')), may hold values from -0.078125 to 0.078125
- w_up: bfloat16 [8, 6144, 8192], P('expert', None, ('dp', 'tensor')), may hold values from -0.078125 to 0.078125
- w_down: bfloat16 [8, 8192, 6144], P('expert', ('dp', 'tensor')), may hold values from -0.0625 to 0.0625
Outputs:
- pool_grad: float32 [512, 6144], P(('dp', 'expert'), 'tensor')
The draws below stay inside these ranges and needn't reach their ends.
Inputs may be any that keep to these rules, and one draw needn't show every extreme that they name: `routes`: in each aligned block of 24 rows (the rows of one sequence) no expert is named by more than 8 rows, a bound that some expert reaches in some or all blocks; the two experts of a row differ.
All inputs are finite; a program needn't handle non-finite values.
Results may differ from the reference program's by a relative error of at most 0.025.
Values may be sent and summed in bfloat16 or wider, within the bound.
A program may use at most 128 MiB of HBM per device.

```python
import math
import jax
import jax.numpy as jnp
import numpy as np
from jax import lax

D = 6144
FF_WIN = 8192
EXPERTS = 8
CAP = 8
PROMPT = 24
TENANTS = 256
SEQS = 32
TOKENS = 768
POOL = 512
N_DP = 4
N_TENSOR = 16


def rising_profile(width, low, high):
    position = jnp.arange(width, dtype=jnp.float32) / max(width - 1, 1)
    return low * jnp.exp(position * jnp.log(high / low))


def draw_pool(key, part):
    key = jax.random.fold_in(key, 11)
    base = jax.random.truncated_normal(key, -6.0, 6.0, (POOL, D), jnp.float32)
    profile = rising_profile(D, 0.4, 4.0)
    return (base * profile[None, :]).astype(jnp.bfloat16)


def draw_norm_gain(key, part):
    key = jax.random.fold_in(key, 23)
    jitter = jax.random.uniform(key, (D,), jnp.float32, 0.85, 1.15)
    profile = rising_profile(D, 0.5, 2.0)
    return (profile * jitter).astype(jnp.bfloat16)


def place_ends(values, rng, least, top_value):
    dims = values.shape
    place = [jax.random.randint(jax.random.fold_in(rng, axis), (), 0, dims[axis]) for axis in range(len(dims))]
    values = values.at[tuple(place)].set(least)
    longest = dims.index(max(dims))
    place[longest] = (place[longest] + 1) % dims[longest]
    return values.at[tuple(place)].set(top_value)


def shard_levels(key, shape, split, smallest, high):
    level = 1.0
    for dim, blocks in split:
        heights = jax.random.uniform(jax.random.fold_in(jax.random.fold_in(key, 6), dim), (blocks,), jnp.float32, smallest / len(split), high / len(split))
        level = level * jnp.repeat(jnp.exp(heights), shape[dim] // blocks).reshape((-1,) + (1,) * (len(shape) - 1 - dim))
    return level


def deal_out(key, own, number, rows, count, top, reach, lean):
    order = jax.random.permutation(key, count)
    heavy_load, ordinary = shares(count, rows * top, reach, lean, True), shares(count, rows * top, reach, lean, False)
    places = jnp.arange(count)

    def named(tallies, rotation):
        used = int((tallies > 0).sum())
        fixed = max(1, used // 4)
        passed = fixed + (places - fixed + rotation * (used - fixed)) % max(1, count - fixed)
        return jnp.zeros((count,), jnp.int32).at[order[jnp.where(places < fixed, places, passed)]].set(jnp.asarray(tallies, jnp.int32))

    tallies = jnp.where(number % 4 == 0, named(heavy_load, number // 4), named(ordinary, number - number // 4 - 1))
    mixed = jax.random.permutation(jax.random.fold_in(own, 3), count)
    donor, sink = mixed[0:count // 2 * 2:2], mixed[1:count // 2 * 2:2]
    slack = jnp.minimum(tallies[donor] - 1, reach - tallies[sink]) // 2
    slack = jnp.where((donor == order[0]) | (sink == order[0]) | (tallies[sink] == 0), 0, jnp.maximum(slack, 0))
    passed = jax.random.randint(jax.random.fold_in(own, 4), (count // 2,), 0, 1 << 20) % (slack + 1)
    tallies = tallies.at[donor].add(-passed).at[sink].add(passed)
    items = jnp.searchsorted(jnp.cumsum(tallies), jnp.arange(rows * top), side="right").astype(jnp.int32)
    listing = items.reshape(top, rows).T
    listing = listing[jax.random.permutation(jax.random.fold_in(own, 1), rows)]
    rotation = jax.random.randint(jax.random.fold_in(own, 2), (rows, 1), 0, top)
    return jnp.take_along_axis(listing, (jnp.arange(top)[None, :] + rotation) % top, axis=1)


def shares(count, total, limit, lean, full):
    loads = [(1 << 20) // math.isqrt(grade ** lean) + 1 for grade in range(1, count + 1)]
    largest = limit if full else min(limit, max(-(-total // count), total * loads[0] // sum(loads)))
    least = 1 if total - largest >= count - 1 else 0
    holding, surplus = [largest] + [least] * (count - 1), total - largest - least * (count - 1)
    while surplus > 0:
        free = [i for i in range(1, count) if holding[i] < largest] or [i for i in range(1, count) if holding[i] < limit]
        whole, left = sum([loads[i] for i in free]), surplus
        for i in free:
            more = min(limit - holding[i], max(1, left * loads[i] // whole), surplus)
            holding[i] = holding[i] + more
            surplus = surplus - more
    return np.array(holding)


def noise(rng, shape, spread, reach, cuts=(), kind=jnp.bfloat16):
    values = jax.random.normal(rng, shape, jnp.float32) * spread
    if len(cuts) > 0:
        values = shard_levels(rng, shape, cuts, -0.22, 0.18) * values
    return jnp.clip(values, min=-reach, max=reach).astype(kind)


def setup_inputs(seed: int = 0) -> dict:
    arg_keys = jax.random.split(jax.random.key(seed), 12)
    pool = draw_pool(jax.random.fold_in(arg_keys[11], 71), 0)
    prompt_ids = place_ends(jax.random.randint(arg_keys[1], (TENANTS, PROMPT), 0, POOL), jax.random.fold_in(arg_keys[1], 1), 0, POOL - 1).astype(jnp.int32)
    tenant = place_ends(jax.random.randint(arg_keys[2], (SEQS,), 0, TENANTS), jax.random.fold_in(arg_keys[2], 1), 0, TENANTS - 1).astype(jnp.int32)
    lengths = place_ends(jax.random.randint(arg_keys[3], (SEQS,), 1, PROMPT + 1), jax.random.fold_in(arg_keys[3], 1), 1, PROMPT).astype(jnp.int32)
    routes_keys = jax.random.split(jax.random.fold_in(arg_keys[4], 1), TOKENS // PROMPT)
    routes_turns = jax.random.permutation(jax.random.fold_in(arg_keys[4], 3), TOKENS // PROMPT)
    routes = jax.vmap(lambda own, number: deal_out(jax.random.fold_in(arg_keys[4], 2), own, number, PROMPT, EXPERTS, 2, CAP, 2))(routes_keys, routes_turns).reshape((TOKENS, 2))
    route_weight = jnp.clip(jnp.exp(math.log(1.0) - 2.3025851 * jax.random.uniform(arg_keys[5], (TOKENS, 2), jnp.float32) ** shard_levels(arg_keys[5], (TOKENS, 2), ((0, 32),), -0.2, 0.2)), 0.1, 1.0)
    cotangent = noise(arg_keys[6], (TOKENS, D), 1.0, 6.0, ((0, 32), (1, 16)))
    norm_gain = draw_norm_gain(jax.random.fold_in(arg_keys[11], 71), 0)
    w_gate = noise(arg_keys[8], (EXPERTS, D, FF_WIN), D ** -0.5, 0.078125, ((0, 8), (2, 64)))
    w_up = noise(arg_keys[9], (EXPERTS, D, FF_WIN), D ** -0.5, 0.078125, ((0, 8), (2, 64)))
    w_down = noise(arg_keys[10], (EXPERTS, FF_WIN, D), FF_WIN ** -0.5, 0.0625, ((0, 8), (1, 64)))
    return dict(pool=pool, prompt_ids=prompt_ids, tenant=tenant, lengths=lengths, routes=routes, route_weight=route_weight, cotangent=cotangent, norm_gain=norm_gain, w_gate=w_gate, w_up=w_up, w_down=w_down)


def reference(pool, prompt_ids, tenant, lengths, routes, route_weight, cotangent, norm_gain, w_gate, w_up, w_down):
    row_ids = prompt_ids[tenant].reshape(-1).astype(jnp.int32)
    rows = pool[row_ids].astype(jnp.float32)
    position = jnp.arange(TOKENS, dtype=jnp.int32) % PROMPT
    live = (position < jnp.repeat(lengths, PROMPT)).astype(jnp.float32)
    masked = cotangent.astype(jnp.float32) * live[:, None]
    gain = norm_gain.astype(jnp.float32)
    scale = lax.rsqrt(lax.optimization_barrier(jnp.mean(rows * rows, axis=1)) + 1e-05)
    normed = (rows * scale[:, None] * gain).astype(jnp.bfloat16)
    expert_cot = (route_weight[:, :, None] * masked[:, None, :]).astype(jnp.bfloat16).reshape(TOKENS * 2, D)
    flat_routes = routes.reshape(-1)
    selected = SEQS * CAP
    hid_block = FF_WIN // (N_DP * N_TENSOR)
    grad_flat = jnp.zeros((TOKENS * 2, D), jnp.float32)
    for expert_id in range(EXPERTS):
        chosen = flat_routes == expert_id
        count = jnp.sum(chosen.astype(jnp.int32))
        index = jnp.nonzero(chosen, size=selected, fill_value=0)[0].astype(jnp.int32)
        valid = (jnp.arange(selected, dtype=jnp.int32) < count).astype(jnp.float32)
        inputs = normed[index // 2]
        cots = (expert_cot[index].astype(jnp.float32) * valid[:, None]).astype(jnp.bfloat16)
        gate_pre = jnp.dot(inputs, w_gate[expert_id], preferred_element_type=jnp.float32)
        up_pre = jnp.dot(inputs, w_up[expert_id], preferred_element_type=jnp.float32)
        back_hidden = jnp.dot(cots, w_down[expert_id].T, preferred_element_type=jnp.float32)
        sigma = jax.nn.sigmoid(gate_pre)
        grad_gate = (back_hidden * up_pre * sigma * (1.0 + gate_pre * (1.0 - sigma))).astype(jnp.bfloat16)
        grad_up = (back_hidden * (gate_pre * sigma)).astype(jnp.bfloat16)
        gate_blocks = grad_gate.reshape(selected, N_DP, N_TENSOR, hid_block)
        up_blocks = grad_up.reshape(selected, N_DP, N_TENSOR, hid_block)
        wg_blocks = w_gate[expert_id].reshape(D, N_DP, N_TENSOR, hid_block)
        wu_blocks = w_up[expert_id].reshape(D, N_DP, N_TENSOR, hid_block)
        total = jnp.zeros((selected, D), jnp.float32)
        for group in range(N_DP):
            terms = jnp.einsum('aih,dih->aid', gate_blocks[:, group].astype(jnp.float32), wg_blocks[:, group].astype(jnp.float32))
            terms = terms + jnp.einsum('aih,dih->aid', up_blocks[:, group].astype(jnp.float32), wu_blocks[:, group].astype(jnp.float32))
            section = lax.optimization_barrier(jnp.sum(terms.astype(jnp.bfloat16).astype(jnp.float32), axis=1))
            total = total + section.astype(jnp.bfloat16).astype(jnp.float32)
        result = total.astype(jnp.bfloat16).astype(jnp.float32) * valid[:, None]
        grad_flat = grad_flat.at[index].add(result)
    row_normed_grad = lax.optimization_barrier(jnp.sum(grad_flat.reshape(TOKENS, 2, D), axis=1))
    weighted = row_normed_grad * gain
    row_dot = lax.optimization_barrier(jnp.sum(weighted * rows, axis=1))
    row_grad = masked + scale[:, None] * weighted - rows * (scale * scale * scale * row_dot / D)[:, None]
    return jnp.zeros((POOL, D), jnp.float32).at[row_ids].add(row_grad)
```

```python
import functools
import heapq

import jax
import jax.numpy as jnp
from jax import lax
from jax.experimental import pallas as pl
from jax.experimental.pallas import tpu as pltpu
from jax.sharding import PartitionSpec as P

D = 6144
EPSILON = 1e-05
MESH = pl.DeviceIdType.MESH
F32, BF16 = jnp.float32, jnp.bfloat16
POOL_ROWS, COT_ROWS, PROMPT = 32, 48, 24
TOKENS = 768
GROUP_ORDER = (2, 1, 3, 0)
NT = (((1,), (1,)), ((), ()))
KEEP = slice(None)


class Net:
    def __init__(self, send_sems, recv_sems):
        self.x = lax.axis_index("dp")
        expert = lax.axis_index("expert")
        tensor = lax.axis_index("tensor")
        self.zl, self.c = expert // 2, expert % 2
        self.zh, self.y = tensor // 4, tensor % 4
        self.z = self.zh * 4 + self.zl
        self.send_sems, self.recv_sems = send_sems, recv_sems
        self.slots = {}
        self.sent = []

    def device(self, x=None, y=None, z=None, c=None):
        x = self.x if x is None else x
        y = self.y if y is None else y
        z = self.z if z is None else z
        c = self.c if c is None else c
        return (x, (z % 4) * 2 + c, (z // 4) * 4 + y)

    def copy(self, key, src, dst, device):
        slot = self.slots.setdefault(key, len(self.slots))
        return pltpu.make_async_remote_copy(
            src_ref=src,
            dst_ref=dst,
            send_sem=self.send_sems.at[slot],
            recv_sem=self.recv_sems.at[slot],
            device_id=device,
            device_id_type=MESH,
        )

    def start(self, key, src, dst, device):
        copy = self.copy(key, src, dst, device)
        copy.start()
        self.sent.append(copy)

    def wait(self, key, dst):
        self.copy(key, dst, dst, self.device(c=1 - self.c)).wait_recv()

    def drain(self):
        for copy in self.sent:
            copy.wait_send()
        self.sent = []


def kind(core, o):
    return "cot" if (core + o) % 2 == 0 else "pool"


ORDERS = ("zyx", "xzy", "yxz")


def region(net, o, done, axis=None, pos=None):
    z = pos if axis == "z" else net.z
    zh, zl = (KEEP, KEEP) if "z" in done else (z // 4, z % 4)
    y = KEEP if "y" in done else (pos if axis == "y" else net.y)
    x = KEEP if "x" in done else (pos if axis == "x" else net.x)
    return (o, zh, y, x, zl)


def gather_order(net, core, o, buf):
    order = ORDERS[o]
    now = 2.0
    done = ""
    for phase, axis in enumerate(order):
        size = 16 if axis == "z" else 4
        me = {"x": net.x, "y": net.y, "z": net.z}[axis]
        last = phase == 2

        def unit(pos, done=done, axis=axis):
            return buf.at[region(net, o, done, axis, pos)]

        def send(step, pos, key, unit=unit, axis=axis, size=size, me=me):
            there = net.device(**{axis: (me + step) % size})
            net.start((o, phase, key), unit(pos), unit(pos), there)

        def to_partner(pos, name, unit=unit):
            net.start((o, "partner", name), unit(pos), unit(pos), net.device(c=1 - net.c))

        if last:
            to_partner(me, 0)
        if not last and axis != "z":
            for step in (2, 1, 3):
                send(step, me, step)
            now += 3.0 if phase == 0 else 4.5
            for step in (1, 3, 2):
                yield now
                net.wait((o, phase, step), unit((me - step) % size))
        else:
            right, left = (size // 2, size // 2 - 1) if core == 0 else (size // 2 - 1, size // 2)
            if axis == "z":
                tick = 3.4 if last else 2.2
            else:
                tick = 9.0
            send(1, me, ("right", 1))
            send(-1, me, ("left", 1))
            for step in range(1, size // 2 + 1):
                now += tick
                for name, sign, count in (("right", 1, right), ("left", -1, left)):
                    if step > count:
                        continue
                    yield now
                    pos = (me - sign * step) % size
                    net.wait((o, phase, (name, step)), unit(pos))
                    if step < count:
                        send(sign, pos, (name, step + 1))
                    if last:
                        to_partner(pos, sign * step)
        done = done + axis


def partner_names(core, o):
    size = 16 if ORDERS[o][2] == "z" else 4
    right, left = (size // 2, size // 2 - 1) if core == 0 else (size // 2 - 1, size // 2)
    names = [0]
    for step in range(1, size // 2 + 1):
        names += [step] if step <= right else []
        names += [-step] if step <= left else []
    return names


def facts_stages(net, facts_ref, facts_got, facts_sum):
    net.start(("facts", 0), facts_ref, facts_got.at[0], net.device(c=1 - net.c))
    yield 3.0
    net.wait(("facts", 0), facts_got.at[0])
    facts_sum[0] = facts_ref[...] + facts_got[0]
    for j in (1, 2, 3):
        there = net.device(z=net.zh * 4 + (net.zl + j) % 4)
        net.start(("facts", j), facts_sum.at[0], facts_got.at[j], there)
    yield 8.5
    for j in (1, 2, 3):
        net.wait(("facts", j), facts_got.at[j])
    facts_sum[1] = facts_sum[0] + facts_got[1] + facts_got[2] + facts_got[3]
    for j in (1, 2, 3):
        there = net.device(x=(net.x + j) % 4)
        net.start(("facts", 3 + j), facts_sum.at[1], facts_got.at[3 + j], there)
    yield 14.5
    for j in (1, 2, 3):
        net.wait(("facts", 3 + j), facts_got.at[3 + j])
    facts_sum[2] = facts_sum[1] + facts_got[4] + facts_got[5] + facts_got[6]


def run_all(tasks):
    heap = []
    for number, task in enumerate(tasks):
        time = next(task, None)
        if time is not None:
            heapq.heappush(heap, (time, number, task))
    while heap:
        _, number, task = heapq.heappop(heap)
        time = next(task, None)
        if time is not None:
            heapq.heappush(heap, (time, number, task))


def gather(net, core, pool_ref, cot_ref, facts_ref, bufs, padded, landed, facts_got, facts_sum):
    partner = net.device(c=1 - net.c)
    here = (net.zh, net.y, net.x, net.zl)
    own_rows = pl.ds(16 * core, 16)
    for o in range(3):
        columns = slice(o * 128, (o + 1) * 128)
        if kind(core, o) == "cot":
            dst = bufs["pool"].at[(o,) + here + (own_rows,)]
            net.start(("swap", o), pool_ref.at[:, pl.ds(o * 128, 128)], dst, partner)
        else:
            block = cot_ref[:, columns].astype(F32)
            padded[o] = jnp.concatenate([block, jnp.zeros((8, 128), F32)], axis=0).astype(BF16)
            net.start(("swap", o), padded.at[o], landed.at[o], partner)
    for o in range(3):
        columns = slice(o * 128, (o + 1) * 128)
        if kind(core, o) == "pool":
            bufs["pool"][(o,) + here + (own_rows,)] = pool_ref[:, columns]
            net.wait(("swap", o), bufs["pool"].at[(o,) + here + (pl.ds(16 * (1 - core), 16),)])
        else:
            net.wait(("swap", o), landed.at[o])
            own = cot_ref[:, columns].astype(F32)
            other = landed[o].astype(F32)[:PROMPT]
            pair = [own, other] if core == 0 else [other, own]
            bufs["cot"][(o,) + here] = jnp.concatenate(pair, axis=0).astype(BF16)
    run_all(
        [gather_order(net, core, o, bufs[kind(core, o)]) for o in range(3)]
        + [facts_stages(net, facts_ref, facts_got, facts_sum)]
    )
    for o in range(3):
        axis = ORDERS[o][2]
        size = 16 if axis == "z" else 4
        me = {"x": net.x, "y": net.y, "z": net.z}[axis]
        buf = bufs[kind(1 - core, o)]
        for name in partner_names(1 - core, o):
            unit = buf.at[region(net, o, ORDERS[o][:2], axis, (me - name) % size)]
            net.wait((o, "partner", name), unit)
    net.drain()


def kernel(
    pool_ref,
    cot_ref,
    facts_ref,
    gain_ref,
    own_gain_ref,
    w_gate_hbm,
    w_up_hbm,
    w_down_hbm,
    out_ref,
    pool_buf,
    cot_buf,
    w_in,
    w_out,
    padded,
    landed,
    facts_got,
    facts_sum,
    hidden,
    back,
    squares,
    scales,
    grads,
    part_out,
    part_in,
    sums,
    first_a,
    first_b,
    mid_a,
    mid_b,
    second_a,
    second_b,
    plane,
    last,
    dot_own,
    dot_pair,
    dot_sum,
    dot_x,
    dot_y,
    dot_z,
    weight_sems,
    send_sems,
    recv_sems,
):
    net = Net(send_sems, recv_sems)
    partner = net.device(c=1 - net.c)
    loads = [
        pltpu.make_async_copy(w_gate_hbm, w_in.at[:, :, pl.ds(0, 128)], weight_sems.at[0]),
        pltpu.make_async_copy(w_up_hbm, w_in.at[:, :, pl.ds(128, 128)], weight_sems.at[1]),
        pltpu.make_async_copy(w_down_hbm, w_out, weight_sems.at[2]),
    ]
    for load in loads:
        load.start()

    barrier = pltpu.get_barrier_semaphore()
    peers = [partner]
    for j in (1, 2, 3):
        peers += [net.device(x=(net.x + j) % 4), net.device(y=(net.y + j) % 4)]
    peers += [net.device(z=(net.z + j) % 16) for j in range(1, 16)]
    for peer in peers:
        pl.semaphore_signal(barrier, inc=1, device_id=peer, device_id_type=MESH)
    pl.semaphore_wait(barrier, len(peers))

    bufs = {"pool": pool_buf, "cot": cot_buf}
    for core in range(2):

        @pl.when(net.c == core)
        def _():
            branch = Net(send_sems, recv_sems)
            branch.slots = net.slots
            gather(
                branch, core, pool_ref, cot_ref, facts_ref, bufs, padded, landed, facts_got, facts_sum
            )

    for load in loads:
        load.wait()

    hidden[...] = jnp.zeros_like(hidden)
    back[...] = jnp.zeros_like(back)
    squares[...] = jnp.zeros_like(squares)
    for o in range(3):

        def columns_step(zh, carry, o=o):
            blocks = [(zh * 4 + y) * 3 + o for y in range(4)]
            normed = []
            square = None
            for y in range(4):
                value = pool_buf[o, zh, y].reshape(16 * POOL_ROWS, 128).astype(F32)
                square = value * value if square is None else square + value * value
                normed.append((value * gain_ref[pl.ds(blocks[y], 1), :]).astype(BF16))
            squares[...] += square
            weights = jnp.concatenate([w_in[b] for b in blocks], axis=0)
            hidden[...] += jnp.dot(
                jnp.concatenate(normed, axis=1), weights, preferred_element_type=F32
            )
            cots = jnp.concatenate(
                [cot_buf[o, zh, y].reshape(TOKENS, 128) for y in range(4)], axis=1
            )
            downs = jnp.concatenate(
                [w_out[:, pl.ds(pl.multiple_of(b * 128, 128), 128)] for b in blocks], axis=1
            )
            back[...] += lax.dot_general(cots, downs, NT, preferred_element_type=F32)
            return carry

        lax.fori_loop(0, 4, columns_step, 0)

    ids = facts_sum[2, 0:1]
    live = facts_sum[2, 1:2]
    expert = (net.zl * 2 + net.c).astype(F32)
    weight = jnp.where(facts_sum[2, 2:3] == expert, facts_sum[2, 4:5], 0.0) + jnp.where(
        facts_sum[2, 3:4] == expert, facts_sum[2, 5:6], 0.0
    )
    back_all = back[...]
    back_hi = back_all.astype(BF16)
    back_lo = (back_all - back_hi.astype(F32)).astype(BF16)

    def rows_step(i, carry):
        rows = pl.ds(pl.multiple_of(i * 128, 128), 128)
        number = (lax.broadcasted_iota(jnp.int32, (128, 1), 0) + i * 128).astype(F32)
        place = jnp.where(ids == number, weight, 0.0)
        place_hi = place.astype(BF16)
        place_lo = (place - place_hi.astype(F32)).astype(BF16)
        got = jnp.dot(place_hi, back_hi, preferred_element_type=F32)
        got += jnp.dot(place_hi, back_lo, preferred_element_type=F32)
        got += jnp.dot(place_lo, back_hi, preferred_element_type=F32)
        scale = lax.rsqrt(jnp.sum(squares[rows], axis=1, keepdims=True) / D + EPSILON)
        scales[rows] = jnp.broadcast_to(scale, (128, 128))
        raw_gate, raw_up = hidden[rows, 0:128], hidden[rows, 128:256]
        gate, up = raw_gate * scale, raw_up * scale
        sigma = jax.nn.sigmoid(gate)
        grad_gate = got * up * sigma * (1.0 + gate * (1.0 - sigma))
        grad_up = got * (gate * sigma)
        both = jnp.concatenate([grad_gate, grad_up], axis=1).astype(BF16).reshape(4, 2, 16, 256)
        half = pl.ds(pl.multiple_of(i * 64, 64), 64)
        grads[0, half] = both[:, 0].reshape(64, 256)
        grads[1, half] = both[:, 1].reshape(64, 256)
        product = grad_gate * raw_gate + grad_up * raw_up
        dot_own[:, rows] = lax.dot_general(
            jnp.ones((8, 128), F32),
            product,
            NT,
            precision=lax.Precision.HIGHEST,
            preferred_element_type=F32,
        )
        return carry

    lax.fori_loop(0, 4, rows_step, 0)

    def product(parity, zh, y):
        weights = jnp.concatenate([w_in[(zh * 4 + y) * 3 + o] for o in range(3)], axis=0)
        return lax.dot_general(grads[parity], weights, NT, preferred_element_type=F32)

    net.start("dot_pair", dot_own, dot_pair, partner)
    spots = [(net.zh + step) % 4 for step in GROUP_ORDER]
    for g, zh in enumerate(spots):

        def other_step(y, carry, zh=zh):
            part_out[zh, y] = product(1 - net.c, zh, y).astype(BF16).reshape(4, 4, 16, 384)
            return carry

        lax.fori_loop(0, 4, other_step, 0)
        net.start(("part", g), part_out.at[zh], part_in.at[zh], partner)

    lanes = [pl.ds(pl.multiple_of((net.x + j) % 4 * 128, 128), 128) for j in range(4)]

    def begin(g):
        zh = spots[g]
        net.wait(("part", g), part_in.at[zh])

        def own_step(y, carry):
            total = product(net.c, zh, y).reshape(4, 4, 16, 384) + part_in[zh, y].astype(F32)
            sums[zh, y] = total.astype(BF16)
            return carry

        lax.fori_loop(0, 4, own_step, 0)
        for j in (2, 1, 3):
            x, y = (net.x + j) % 4, (net.y + j) % 4
            net.start(
                ("a1", g, j), sums.at[zh, :, x, pl.ds(0, 2)], first_a.at[g, j - 1], net.device(x=x)
            )
            net.start(
                ("b1", g, j), sums.at[zh, y, :, pl.ds(2, 2)], first_b.at[g, j - 1], net.device(y=y)
            )

    def middle(g):
        zh = spots[g]
        for j in (1, 2, 3):
            net.wait(("a1", g, j), first_a.at[g, j - 1])
            net.wait(("b1", g, j), first_b.at[g, j - 1])
        own_a = sums[zh, :, net.x, 0:2].astype(F32)
        own_b = sums[zh, net.y, :, 2:4].astype(F32)
        for j in range(3):
            own_a += first_a[g, j].astype(F32)
            own_b += first_b[g, j].astype(F32)
        mid_a[g] = own_a.astype(BF16)
        mid_b[g] = own_b.astype(BF16)
        for j in (2, 1, 3):
            x, y = (net.x + j) % 4, (net.y + j) % 4
            net.start(("a2", g, j), mid_a.at[g, y], second_a.at[g, j - 1], net.device(y=y))
            net.start(("b2", g, j), mid_b.at[g, x], second_b.at[g, j - 1], net.device(x=x))

    def finish(g):
        step = GROUP_ORDER[g]
        for j in (1, 2, 3):
            net.wait(("a2", g, j), second_a.at[g, j - 1])
            net.wait(("b2", g, j), second_b.at[g, j - 1])
        own_a = mid_a[g, net.y].astype(F32)
        own_b = mid_b[g, net.x].astype(F32)
        for j in range(3):
            own_a += second_a[g, j].astype(F32)
            own_b += second_b[g, j].astype(F32)
        plane[g, 0:2] = own_a.astype(BF16)
        plane[g, 2:4] = own_b.astype(BF16)
        for j in range(4):
            if step == 0 and j == 0:
                continue
            zl = (net.zl + j) % 4
            slot = step * 4 + j
            net.start(
                ("z", slot), plane.at[g, zl], last.at[slot], net.device(z=spots[g] * 4 + zl)
            )

    def dot_one():
        net.wait("dot_pair", dot_pair)
        dot_sum[...] = dot_own[...] + dot_pair[...]
        for j in (1, 2, 3):
            net.start(
                ("dot_x", j), dot_sum.at[:, lanes[j]], dot_x.at[j], net.device(x=(net.x + j) % 4)
            )

    def dot_two():
        for j in (1, 2, 3):
            net.wait(("dot_x", j), dot_x.at[j])
        dot_y[0] = dot_sum[:, lanes[0]] + dot_x[1] + dot_x[2] + dot_x[3]
        for j in (1, 2, 3):
            net.start(("dot_y", j), dot_y.at[0], dot_y.at[j], net.device(y=(net.y + j) % 4))

    def dot_three():
        for j in (1, 2, 3):
            net.wait(("dot_y", j), dot_y.at[j])
        dot_z[0] = dot_y[0] + dot_y[1] + dot_y[2] + dot_y[3]
        for j in range(1, 16):
            net.start(("dot_z", j), dot_z.at[0], dot_z.at[j], net.device(z=(net.z + j) % 16))

    begin(0)
    dot_one()
    begin(1)
    middle(0)
    dot_two()
    begin(2)
    middle(1)
    dot_three()
    finish(0)
    begin(3)
    middle(2)
    finish(1)

    first = ((net.x * 4 + net.zl) * 2 + net.c) * 16
    own_number = (lax.broadcasted_iota(jnp.int32, (16, 1), 0) + first).astype(F32)
    own_place = jnp.where(ids == own_number, live, 0.0).astype(BF16)
    direct = jnp.concatenate(
        [
            jnp.dot(
                own_place,
                cot_buf[o, net.zh, net.y].reshape(TOKENS, 128),
                preferred_element_type=F32,
            )
            for o in range(3)
        ],
        axis=1,
    )

    middle(3)
    finish(2)
    finish(3)

    for j in range(1, 16):
        net.wait(("dot_z", j), dot_z.at[j])
    dots = dot_z[0]
    for j in range(1, 16):
        dots += dot_z[j]
    own_lane = (net.zl * 2 + net.c) * 16 + lax.broadcasted_iota(jnp.int32, (16, 128), 0)
    picked = jnp.where(lax.broadcasted_iota(jnp.int32, (16, 128), 1) == own_lane, dots[0:1], 0.0)
    own_dot = jnp.sum(picked, axis=1, keepdims=True)
    scale = scales[pl.ds(pl.multiple_of(first, 16), 16), 0:1]
    factor = scale * scale * scale * own_dot / D

    total = plane[3, net.zl].astype(F32)
    for step in GROUP_ORDER:
        for j in range(4):
            slot = step * 4 + j
            if slot > 0:
                net.wait(("z", slot), last.at[slot])
                total += last[slot].astype(F32)
    out_ref[...] = (
        direct + scale * own_gain_ref[...] * total - pool_ref[...].astype(F32) * factor
    )
    net.drain()


def local(
    pool,
    prompt_ids,
    tenant,
    lengths,
    routes,
    route_weight,
    cotangent,
    norm_gain,
    w_gate,
    w_up,
    w_down,
):
    sequence = lax.axis_index(("dp", "expert"))
    ids = prompt_ids[tenant[0]]
    live = (jnp.arange(PROMPT, dtype=jnp.int32) < lengths[0]).astype(F32)
    facts = jnp.concatenate(
        [
            ids[None].astype(F32),
            live[None],
            routes.T.astype(F32),
            route_weight.T * live[None],
            jnp.zeros((2, PROMPT), F32),
        ],
        axis=0,
    )
    facts = lax.dynamic_update_slice(
        jnp.zeros((8, TOKENS), F32), facts, (0, sequence * PROMPT)
    )
    gain = norm_gain.astype(F32).reshape(48, 128)
    own_gain = lax.dynamic_slice_in_dim(
        norm_gain.astype(F32), lax.axis_index("tensor") * 384, 384, 0
    ).reshape(1, 384)
    vmem = pl.BlockSpec(memory_space=pltpu.VMEM)
    hbm = pl.BlockSpec(memory_space=pl.ANY)
    sums_shape = pltpu.VMEM((4, 4, 4, 4, 16, 384), BF16)
    copies = 200
    return pl.pallas_call(
        kernel,
        out_shape=jax.ShapeDtypeStruct((16, 384), F32),
        in_specs=[vmem] * 5 + [hbm] * 3,
        out_specs=vmem,
        scratch_shapes=[
            pltpu.VMEM((3, 4, 4, 4, 4, POOL_ROWS, 128), BF16),
            pltpu.VMEM((3, 4, 4, 4, 4, COT_ROWS, 128), BF16),
            pltpu.VMEM((48, 128, 256), BF16),
            pltpu.VMEM((128, D), BF16),
            pltpu.VMEM((3, 32, 128), BF16),
            pltpu.VMEM((3, 32, 128), BF16),
            pltpu.VMEM((7, 8, TOKENS), F32),
            pltpu.VMEM((3, 8, TOKENS), F32),
            pltpu.VMEM((512, 256), F32),
            pltpu.VMEM((TOKENS, 128), F32),
            pltpu.VMEM((512, 128), F32),
            pltpu.VMEM((512, 128), F32),
            pltpu.VMEM((2, 256, 256), BF16),
            sums_shape,
            sums_shape,
            sums_shape,
            pltpu.VMEM((4, 3, 4, 2, 16, 384), BF16),
            pltpu.VMEM((4, 3, 4, 2, 16, 384), BF16),
            pltpu.VMEM((4, 4, 2, 16, 384), BF16),
            pltpu.VMEM((4, 4, 2, 16, 384), BF16),
            pltpu.VMEM((4, 3, 2, 16, 384), BF16),
            pltpu.VMEM((4, 3, 2, 16, 384), BF16),
            pltpu.VMEM((4, 4, 16, 384), BF16),
            pltpu.VMEM((16, 16, 384), BF16),
            pltpu.VMEM((8, 512), F32),
            pltpu.VMEM((8, 512), F32),
            pltpu.VMEM((8, 512), F32),
            pltpu.VMEM((4, 8, 128), F32),
            pltpu.VMEM((4, 8, 128), F32),
            pltpu.VMEM((16, 8, 128), F32),
            pltpu.SemaphoreType.DMA((3,)),
            pltpu.SemaphoreType.DMA((copies,)),
            pltpu.SemaphoreType.DMA((copies,)),
        ],
        compiler_params=pltpu.CompilerParams(
            collective_id=0, has_side_effects=True, vmem_limit_bytes=56 * 2**20
        ),
        name="moe_backward",
    )(
        pool,
        cotangent,
        facts,
        gain,
        own_gain,
        w_gate.reshape(48, 128, 128),
        w_up.reshape(48, 128, 128),
        w_down[0],
    )


def solution(mesh):
    placed = (
        P(("dp", "expert"), "tensor"),
        P(),
        P(("dp", "expert")),
        P(("dp", "expert")),
        P(("dp", "expert"), None),
        P(("dp", "expert"), None),
        P(("dp", "expert"), "tensor"),
        P(),
        P("expert", None, ("dp", "tensor")),
        P("expert", None, ("dp", "tensor")),
        P("expert", ("dp", "tensor"), None),
    )
    return jax.shard_map(
        local, mesh=mesh, in_specs=placed, out_specs=P(("dp", "expert"), "tensor"), check_vma=False
    )
```

```python
import jax
import jax.numpy as jnp
from jax import lax
from jax.experimental import pallas as pl
from jax.experimental.pallas import tpu as pltpu
from jax.sharding import PartitionSpec as P

D = 6144
EPSILON = 1e-05
MESH = pl.DeviceIdType.MESH
F32, BF16 = jnp.float32, jnp.bfloat16
POOL_ROWS, COT_ROWS, PROMPT = 32, 48, 24
TOKENS = 768
GROUP_ORDER = (2, 1, 3, 0)
NT = (((1,), (1,)), ((), ()))
KEEP = slice(None)


class Net:
    def __init__(self, send_sems, recv_sems):
        self.x = lax.axis_index("dp")
        expert = lax.axis_index("expert")
        tensor = lax.axis_index("tensor")
        self.zl, self.c = expert // 2, expert % 2
        self.zh, self.y = tensor // 4, tensor % 4
        self.z = self.zh * 4 + self.zl
        self.send_sems, self.recv_sems = send_sems, recv_sems
        self.slots = {}
        self.sent = {}

    def device(self, x=None, y=None, z=None, c=None):
        x = self.x if x is None else x
        y = self.y if y is None else y
        z = self.z if z is None else z
        c = self.c if c is None else c
        return (x, (z % 4) * 2 + c, (z // 4) * 4 + y)

    def copy(self, key, src, dst, device):
        slot = self.slots.setdefault(key, len(self.slots))
        assert slot < Slots.STATIC
        return self.copy_at(slot, src, dst, device)

    def copy_at(self, slot, src, dst, device):
        return pltpu.make_async_remote_copy(
            src_ref=src,
            dst_ref=dst,
            send_sem=self.send_sems.at[slot],
            recv_sem=self.recv_sems.at[slot],
            device_id=device,
            device_id_type=MESH,
        )

    def start(self, key, src, dst, device):
        copy = self.copy(key, src, dst, device)
        copy.start()
        self.sent[key] = copy

    def wait(self, key, dst):
        self.copy(key, dst, dst, self.device(c=1 - self.c)).wait_recv()

    def drain(self):
        for copy in self.sent.values():
            copy.wait_send()
        self.sent = {}

    def drain_sizes(self, sizes, stand_in):
        for key, shape, dtype in sizes:
            ref = stand_in(shape, dtype)
            self.copy(key, ref, ref, self.device(c=1 - self.c)).wait_send()


def kind(core, o):
    return "cot" if (core + o) % 2 == 0 else "pool"


def spot(o, z, y, x):
    zh, zl = (KEEP, KEEP) if z is None else (z // 4, z % 4)
    return (o, zh, KEEP if y is None else y, KEEP if x is None else x, zl)


def ring_steps(core, size):
    return (size // 2, size // 2 - 1) if core == 0 else (size // 2 - 1, size // 2)


class Slots:
    STATIC = 110
    LINE = STATIC
    PLANE = LINE + 6 * 18
    HAND = PLANE + 2 * 16 * 7
    COUNT = HAND + 3 * 16

    @staticmethod
    def line(number, sign, step):
        return Slots.LINE + number * 18 + (0 if sign == 1 else 9) + step

    @staticmethod
    def plane(o, distance, which):
        return Slots.PLANE + (o * 16 + distance) * 7 + which

    @staticmethod
    def hand(o, distance):
        return Slots.HAND + o * 16 + distance


class Gather:
    def __init__(self, net, core, bufs):
        self.net, self.core, self.bufs = net, core, bufs
        right, left = ring_steps(core, 16)
        self.signs = ((1, 0, right), (-1, 1, left))
        self.long = 1 if core == 0 else -1

    def unit(self, o, z, y, x):
        return self.bufs[kind(self.core, o)].at[spot(o, z, y, x)]

    def send(self, slot, unit, device):
        self.net.copy_at(slot, unit, unit, device).start()

    def wait(self, slot, unit):
        self.net.copy_at(slot, unit, unit, self.net.device(c=1 - self.net.c)).wait_recv()

    def wait_sent(self, slot, unit):
        self.net.copy_at(slot, unit, unit, self.net.device(c=1 - self.net.c)).wait_send()

    def distance(self, sign, step):
        return (16 - step) % 16 if sign == 1 else step % 16

    def line_unit(self, number, pos):
        net = self.net
        if number < 2:
            return self.unit(number, pos, net.y, net.x)
        return self.unit(2, pos, None, (net.x - (number - 2)) % 4)

    def line_send(self, number, sign, step):
        net = self.net
        unit = self.line_unit(number, (net.z + 16 - sign * (step - 1)) % 16)
        self.send(Slots.line(number, sign, step), unit, net.device(z=(net.z + 16 + sign) % 16))

    def line_step(self, number, sign, count, step):
        unit = self.line_unit(number, (self.net.z + 16 - sign * step) % 16)
        self.wait(Slots.line(number, sign, step), unit)

        @pl.when(step < count)
        def _():
            self.line_send(number, sign, step + 1)

    def one(self, o, z, step):
        net = self.net
        if o == 0:
            return self.unit(o, z, (net.y + step) % 4, net.x)
        return self.unit(o, z, net.y, (net.x + step) % 4)

    def two(self, o, z, step):
        net = self.net
        if o == 0:
            return self.unit(o, z, None, (net.x + step) % 4)
        return self.unit(o, z, (net.y + step) % 4, None)

    def along(self, o, ring, step):
        net = self.net
        if (o == 0) == (ring == 0):
            return net.device(y=(net.y + step) % 4)
        return net.device(x=(net.x + step) % 4)

    def plane_start(self, o, sign, step):
        d = self.distance(sign, step)
        z = (self.net.z + d) % 16
        for j in (2, 1, 3):
            self.send(Slots.plane(o, d, j - 1), self.one(o, z, 0), self.along(o, 0, j))

    def plane_turn(self, o, sign, step):
        d = self.distance(sign, step)
        z = (self.net.z + d) % 16
        for j in (1, 3, 2):
            self.wait(Slots.plane(o, d, j - 1), self.one(o, z, 4 - j))
        for slot, way in ((3, self.long), (4, -self.long)):
            self.send(Slots.plane(o, d, slot), self.two(o, z, 0), self.along(o, 1, 4 + way))

    def plane_pass(self, o, sign, step):
        d = self.distance(sign, step)
        z = (self.net.z + d) % 16
        self.wait(Slots.plane(o, d, 3), self.two(o, z, 4 - self.long))
        self.send(
            Slots.plane(o, d, 5), self.two(o, z, 4 - self.long), self.along(o, 1, 4 + self.long)
        )
        self.wait(Slots.plane(o, d, 4), self.two(o, z, 4 + self.long))

    def plane_end(self, o, sign, step):
        d = self.distance(sign, step)
        z = (self.net.z + d) % 16
        self.wait(Slots.plane(o, d, 5), self.two(o, z, 2))
        self.hand_over(o, d)

    def hand_over(self, o, d):
        net = self.net
        unit = self.unit(o, (net.z + d) % 16, None, None)
        self.send(Slots.hand(o, d), unit, net.device(c=1 - net.c))

    def begin(self):
        net = self.net
        for number in (0, 1):
            self.line_send(number, 1, 1)
            self.line_send(number, -1, 1)
        own = self.unit(2, net.z, net.y, net.x)
        for j in (2, 1, 3):
            net.start(("y", j), own, own, net.device(y=(net.y + j) % 4))

    def own_line(self):
        net = self.net
        for j in (1, 3, 2):
            net.wait(("y", j), self.unit(2, net.z, (net.y + 4 - j) % 4, net.x))
        self.line_send(2, 1, 1)
        self.line_send(2, -1, 1)
        own = self.unit(2, net.z, None, net.x)
        for j in (2, 1, 3):
            net.start(("x", j), own, own, net.device(x=(net.x + j) % 4))

    def other_lines(self):
        net = self.net
        for j in (1, 3, 2):
            net.wait(("x", j), self.unit(2, net.z, None, (net.x + 4 - j) % 4))
            self.line_send(2 + j, 1, 1)
            self.line_send(2 + j, -1, 1)
        self.hand_over(2, 0)

    def steps(self, s, facts):
        for sign, first, count in self.signs:

            @pl.when((s >= 1) & (s <= count))
            def _():
                self.line_step(0, sign, count, s)
                self.line_step(1, sign, count, s)

            @pl.when((s >= first) & (s <= count))
            def _():
                self.plane_start(0, sign, s)
                self.plane_start(1, sign, s)

        pl.when(s == 1)(self.own_line)
        pl.when(s == 2)(self.other_lines)
        for sign, first, count in self.signs:

            @pl.when((s >= 3) & (s - 2 <= count))
            def _():
                for number in range(2, 6):
                    self.line_step(number, sign, count, s - 2)
                self.hand_over(2, self.distance(sign, s - 2))

        for late, stage in ((1, self.plane_turn), (2, self.plane_pass), (3, self.plane_end)):
            for sign, first, count in self.signs:

                @pl.when((s >= late + first) & (s - late <= count))
                def _():
                    stage(0, sign, s - late)
                    stage(1, sign, s - late)

        for number, stage in enumerate(facts):
            pl.when(s == 2 + 2 * number)(stage)

    def run(self, facts):
        def body(s, carry):
            self.steps(s, facts)
            return carry

        self.begin()
        lax.fori_loop(0, 12, body, 0)

        def landed(d, carry):
            for o in range(3):
                other = self.bufs[kind(1 - self.core, o)]
                self.wait(Slots.hand(o, d), other.at[spot(o, (self.net.z + d) % 16, None, None)])
            return carry

        lax.fori_loop(0, 16, landed, 0)

    def drain(self):
        def blocks(d, carry):
            for o in (0, 1):
                for which in range(3):
                    self.wait_sent(Slots.plane(o, d, which), self.unit(o, 0, 0, 0))
                for which in range(3, 6):
                    self.wait_sent(Slots.plane(o, d, which), self.unit(o, 0, None, 0))
            for o in range(3):
                self.wait_sent(Slots.hand(o, d), self.unit(o, 0, None, None))
            return carry

        lax.fori_loop(0, 16, blocks, 0)
        for sign, _, count in self.signs:

            def lines(step, carry, sign=sign):
                for number in range(6):
                    unit = self.unit(min(number, 2), 0, 0 if number < 2 else None, 0)
                    self.wait_sent(Slots.line(number, sign, step), unit)
                return carry

            lax.fori_loop(1, count + 1, lines, 0)


def facts_stages(net, facts_ref, facts_got, facts_sum):
    net.start(("facts", 0), facts_ref, facts_got.at[0], net.device(c=1 - net.c))

    def pair():
        net.wait(("facts", 0), facts_got.at[0])
        facts_sum[0] = facts_ref[...] + facts_got[0]
        for j in (1, 2, 3):
            there = net.device(z=net.zh * 4 + (net.zl + j) % 4)
            net.start(("facts", j), facts_sum.at[0], facts_got.at[j], there)

    def near():
        for j in (1, 2, 3):
            net.wait(("facts", j), facts_got.at[j])
        facts_sum[1] = facts_sum[0] + facts_got[1] + facts_got[2] + facts_got[3]
        for j in (1, 2, 3):
            there = net.device(x=(net.x + j) % 4)
            net.start(("facts", 3 + j), facts_sum.at[1], facts_got.at[3 + j], there)

    def whole():
        for j in (1, 2, 3):
            net.wait(("facts", 3 + j), facts_got.at[3 + j])
        facts_sum[2] = facts_sum[1] + facts_got[4] + facts_got[5] + facts_got[6]

    return pair, near, whole


def gather(net, core, pool_ref, cot_ref, facts_ref, bufs, padded, landed, facts_got, facts_sum):
    partner = net.device(c=1 - net.c)
    here = (net.zh, net.y, net.x, net.zl)
    own_rows = pl.ds(16 * core, 16)
    for o in range(3):
        columns = slice(o * 128, (o + 1) * 128)
        if kind(core, o) == "cot":
            dst = bufs["pool"].at[(o,) + here + (own_rows,)]
            net.start(("swap", o), pool_ref.at[:, pl.ds(o * 128, 128)], dst, partner)
        else:
            block = cot_ref[:, columns].astype(F32)
            padded[o] = jnp.concatenate([block, jnp.zeros((8, 128), F32)], axis=0).astype(BF16)
            net.start(("swap", o), padded.at[o], landed.at[o], partner)
    for o in range(3):
        columns = slice(o * 128, (o + 1) * 128)
        if kind(core, o) == "pool":
            bufs["pool"][(o,) + here + (own_rows,)] = pool_ref[:, columns]
            net.wait(("swap", o), bufs["pool"].at[(o,) + here + (pl.ds(16 * (1 - core), 16),)])
        else:
            net.wait(("swap", o), landed.at[o])
            own = cot_ref[:, columns].astype(F32)
            other = landed[o].astype(F32)[:PROMPT]
            pair = [own, other] if core == 0 else [other, own]
            bufs["cot"][(o,) + here] = jnp.concatenate(pair, axis=0).astype(BF16)
    work = Gather(net, core, bufs)
    work.run(facts_stages(net, facts_ref, facts_got, facts_sum))
    return [(key, copy.src_ref.shape, copy.src_ref.dtype) for key, copy in net.sent.items()]


def kernel(
    pool_ref,
    cot_ref,
    facts_ref,
    gain_ref,
    w_gate_hbm,
    w_up_hbm,
    w_down_hbm,
    out_ref,
    pool_buf,
    cot_buf,
    w_in,
    w_out,
    padded,
    landed,
    facts_got,
    facts_sum,
    hidden,
    back,
    squares,
    scales,
    grads,
    part_out,
    part_in,
    sums,
    first_a,
    first_b,
    mid_a,
    mid_b,
    second_a,
    second_b,
    plane,
    last,
    dot_own,
    dot_pair,
    dot_sum,
    dot_x,
    dot_y,
    dot_z,
    gain_all,
    weight_sems,
    send_sems,
    recv_sems,
):
    gain_all[...] = gain_ref[...].astype(F32)
    net = Net(send_sems, recv_sems)
    partner = net.device(c=1 - net.c)
    loads = [
        pltpu.make_async_copy(w_gate_hbm, w_in.at[:, :, pl.ds(0, 128)], weight_sems.at[0]),
        pltpu.make_async_copy(w_up_hbm, w_in.at[:, :, pl.ds(128, 128)], weight_sems.at[1]),
        pltpu.make_async_copy(w_down_hbm, w_out, weight_sems.at[2]),
    ]
    for load in loads:
        load.start()

    barrier = pltpu.get_barrier_semaphore()
    peers = [partner]
    for j in (1, 2, 3):
        peers += [net.device(x=(net.x + j) % 4), net.device(y=(net.y + j) % 4)]
    peers += [net.device(z=(net.z + j) % 16) for j in range(1, 16)]
    for peer in peers:
        pl.semaphore_signal(barrier, inc=1, device_id=peer, device_id_type=MESH)
    pl.semaphore_wait(barrier, len(peers))

    bufs = {"pool": pool_buf, "cot": cot_buf}
    sizes = [None, None]
    for core in range(2):

        @pl.when(net.c == core)
        def _():
            branch = Net(send_sems, recv_sems)
            branch.slots = net.slots
            sizes[core] = gather(
                branch, core, pool_ref, cot_ref, facts_ref, bufs, padded, landed, facts_got, facts_sum
            )

    for load in loads:
        load.wait()

    def stand_in(shape, dtype):
        if dtype == F32:
            return facts_sum.at[0]
        if shape == (16, 128):
            return padded.at[0, pl.ds(0, 16)]
        if shape == (32, 128):
            return padded.at[0]
        buf = pool_buf if shape[-2] == POOL_ROWS else cot_buf
        ref = buf.at[(0,) * (7 - len(shape))]
        assert ref.shape == shape
        return ref

    def drain_gather():
        for core in range(2):

            @pl.when(net.c == core)
            def _():
                net.drain_sizes(sizes[core], stand_in)
                Gather(net, core, bufs).drain()

    hidden[...] = jnp.zeros_like(hidden)
    back[...] = jnp.zeros_like(back)
    squares[...] = jnp.zeros_like(squares)
    for o in range(3):

        def columns_step(zh, carry, o=o):
            blocks = [(zh * 4 + y) * 3 + o for y in range(4)]
            normed = []
            square = None
            for y in range(4):
                value = pool_buf[o, zh, y].reshape(16 * POOL_ROWS, 128).astype(F32)
                square = value * value if square is None else square + value * value
                normed.append((value * gain_all[pl.ds(blocks[y], 1), :]).astype(BF16))
            squares[...] += square
            weights = jnp.concatenate([w_in[b] for b in blocks], axis=0)
            hidden[...] += jnp.dot(
                jnp.concatenate(normed, axis=1), weights, preferred_element_type=F32
            )
            cots = jnp.concatenate(
                [cot_buf[o, zh, y].reshape(TOKENS, 128) for y in range(4)], axis=1
            )
            downs = jnp.concatenate(
                [w_out[:, pl.ds(pl.multiple_of(b * 128, 128), 128)] for b in blocks], axis=1
            )
            back[...] += lax.dot_general(cots, downs, NT, preferred_element_type=F32)
            return carry

        lax.fori_loop(0, 4, columns_step, 0)

    ids = facts_sum[2, 0:1]
    live = facts_sum[2, 1:2]
    expert = (net.zl * 2 + net.c).astype(F32)
    weight = jnp.where(facts_sum[2, 2:3] == expert, facts_sum[2, 4:5], 0.0) + jnp.where(
        facts_sum[2, 3:4] == expert, facts_sum[2, 5:6], 0.0
    )
    back_all = back[...]
    back_hi = back_all.astype(BF16)
    back_lo = (back_all - back_hi.astype(F32)).astype(BF16)

    def rows_step(i, carry):
        rows = pl.ds(pl.multiple_of(i * 128, 128), 128)
        number = (lax.broadcasted_iota(jnp.int32, (128, 1), 0) + i * 128).astype(F32)
        place = jnp.where(ids == number, weight, 0.0)
        place_hi = place.astype(BF16)
        place_lo = (place - place_hi.astype(F32)).astype(BF16)
        got = jnp.dot(place_hi, back_hi, preferred_element_type=F32)
        got += jnp.dot(place_hi, back_lo, preferred_element_type=F32)
        got += jnp.dot(place_lo, back_hi, preferred_element_type=F32)
        scale = lax.rsqrt(jnp.sum(squares[rows], axis=1, keepdims=True) / D + EPSILON)
        scales[rows] = jnp.broadcast_to(scale, (128, 128))
        raw_gate, raw_up = hidden[rows, 0:128], hidden[rows, 128:256]
        gate, up = raw_gate * scale, raw_up * scale
        sigma = jax.nn.sigmoid(gate)
        grad_gate = got * up * sigma * (1.0 + gate * (1.0 - sigma))
        grad_up = got * (gate * sigma)
        both = jnp.concatenate([grad_gate, grad_up], axis=1).astype(BF16).reshape(4, 2, 16, 256)
        half = pl.ds(pl.multiple_of(i * 64, 64), 64)
        grads[0, half] = both[:, 0].reshape(64, 256)
        grads[1, half] = both[:, 1].reshape(64, 256)
        product = grad_gate * raw_gate + grad_up * raw_up
        dot_own[:, rows] = lax.dot_general(
            jnp.ones((8, 128), F32),
            product,
            NT,
            precision=lax.Precision.HIGHEST,
            preferred_element_type=F32,
        )
        return carry

    lax.fori_loop(0, 4, rows_step, 0)

    def product(parity, zh, y):
        weights = jnp.concatenate([w_in[(zh * 4 + y) * 3 + o] for o in range(3)], axis=0)
        return lax.dot_general(grads[parity], weights, NT, preferred_element_type=F32)

    net.start("dot_pair", dot_own, dot_pair, partner)
    spots = [(net.zh + step) % 4 for step in GROUP_ORDER]

    def other(g):
        zh = spots[g]

        def other_step(y, carry):
            part_out[zh, y] = product(1 - net.c, zh, y).astype(BF16).reshape(4, 4, 16, 384)
            return carry

        lax.fori_loop(0, 4, other_step, 0)
        net.start(("part", g), part_out.at[zh], part_in.at[zh], partner)

    lanes = [pl.ds(pl.multiple_of((net.x + j) % 4 * 128, 128), 128) for j in range(4)]

    def begin(g):
        zh = spots[g]
        net.wait(("part", g), part_in.at[zh])

        def own_step(y, carry):
            total = product(net.c, zh, y).reshape(4, 4, 16, 384) + part_in[zh, y].astype(F32)
            sums[zh, y] = total.astype(BF16)
            return carry

        lax.fori_loop(0, 4, own_step, 0)
        for j in (2, 1, 3):
            x, y = (net.x + j) % 4, (net.y + j) % 4
            net.start(
                ("a1", g, j), sums.at[zh, :, x, pl.ds(0, 2)], first_a.at[g, j - 1], net.device(x=x)
            )
            net.start(
                ("b1", g, j), sums.at[zh, y, :, pl.ds(2, 2)], first_b.at[g, j - 1], net.device(y=y)
            )

    def middle(g):
        zh = spots[g]
        for j in (1, 2, 3):
            net.wait(("a1", g, j), first_a.at[g, j - 1])
            net.wait(("b1", g, j), first_b.at[g, j - 1])
        own_a = sums[zh, :, net.x, 0:2].astype(F32)
        own_b = sums[zh, net.y, :, 2:4].astype(F32)
        for j in range(3):
            own_a += first_a[g, j].astype(F32)
            own_b += first_b[g, j].astype(F32)
        mid_a[g] = own_a.astype(BF16)
        mid_b[g] = own_b.astype(BF16)
        for j in (2, 1, 3):
            x, y = (net.x + j) % 4, (net.y + j) % 4
            net.start(("a2", g, j), mid_a.at[g, y], second_a.at[g, j - 1], net.device(y=y))
            net.start(("b2", g, j), mid_b.at[g, x], second_b.at[g, j - 1], net.device(x=x))

    def finish(g):
        step = GROUP_ORDER[g]
        for j in (1, 2, 3):
            net.wait(("a2", g, j), second_a.at[g, j - 1])
            net.wait(("b2", g, j), second_b.at[g, j - 1])
        own_a = mid_a[g, net.y].astype(F32)
        own_b = mid_b[g, net.x].astype(F32)
        for j in range(3):
            own_a += second_a[g, j].astype(F32)
            own_b += second_b[g, j].astype(F32)
        plane[g, 0:2] = own_a.astype(BF16)
        plane[g, 2:4] = own_b.astype(BF16)
        for j in range(4):
            if step == 0 and j == 0:
                continue
            zl = (net.zl + j) % 4
            slot = step * 4 + j
            net.start(
                ("z", slot), plane.at[g, zl], last.at[slot], net.device(z=spots[g] * 4 + zl)
            )

    def dot_one():
        net.wait("dot_pair", dot_pair)
        dot_sum[...] = dot_own[...] + dot_pair[...]
        for j in (1, 2, 3):
            net.start(
                ("dot_x", j), dot_sum.at[:, lanes[j]], dot_x.at[j], net.device(x=(net.x + j) % 4)
            )

    def dot_two():
        for j in (1, 2, 3):
            net.wait(("dot_x", j), dot_x.at[j])
        dot_y[0] = dot_sum[:, lanes[0]] + dot_x[1] + dot_x[2] + dot_x[3]
        for j in (1, 2, 3):
            net.start(("dot_y", j), dot_y.at[0], dot_y.at[j], net.device(y=(net.y + j) % 4))

    def dot_three():
        for j in (1, 2, 3):
            net.wait(("dot_y", j), dot_y.at[j])
        dot_z[0] = dot_y[0] + dot_y[1] + dot_y[2] + dot_y[3]
        for j in range(1, 16):
            net.start(("dot_z", j), dot_z.at[0], dot_z.at[j], net.device(z=(net.z + j) % 16))

    other(0)
    other(1)
    begin(0)
    dot_one()
    other(2)
    begin(1)
    dot_two()
    middle(0)
    other(3)
    begin(2)
    dot_three()
    middle(1)
    finish(0)
    begin(3)
    middle(2)
    finish(1)

    first = ((net.x * 4 + net.zl) * 2 + net.c) * 16
    own_number = (lax.broadcasted_iota(jnp.int32, (16, 1), 0) + first).astype(F32)
    own_place = jnp.where(ids == own_number, live, 0.0).astype(BF16)
    direct = jnp.concatenate(
        [
            jnp.dot(
                own_place,
                cot_buf[o, net.zh, net.y].reshape(TOKENS, 128),
                preferred_element_type=F32,
            )
            for o in range(3)
        ],
        axis=1,
    )

    middle(3)
    finish(2)
    finish(3)

    for j in range(1, 16):
        net.wait(("dot_z", j), dot_z.at[j])
    dots = dot_z[0]
    for j in range(1, 16):
        dots += dot_z[j]
    own_lane = (net.zl * 2 + net.c) * 16 + lax.broadcasted_iota(jnp.int32, (16, 128), 0)
    picked = jnp.where(lax.broadcasted_iota(jnp.int32, (16, 128), 1) == own_lane, dots[0:1], 0.0)
    own_dot = jnp.sum(picked, axis=1, keepdims=True)
    scale = scales[pl.ds(pl.multiple_of(first, 16), 16), 0:1]
    factor = scale * scale * scale * own_dot / D

    tile = (net.zh * 4 + net.y) * 3
    own_gain = jnp.concatenate([gain_all[pl.ds(tile + o, 1), :] for o in range(3)], axis=1)
    total = plane[3, net.zl].astype(F32)
    for step in GROUP_ORDER:
        for j in range(4):
            slot = step * 4 + j
            if slot > 0:
                net.wait(("z", slot), last.at[slot])
                total += last[slot].astype(F32)
    out_ref[...] = (
        direct + scale * own_gain * total - pool_ref[...].astype(F32) * factor
    )
    net.drain()
    drain_gather()


def local(
    pool,
    prompt_ids,
    tenant,
    lengths,
    routes,
    route_weight,
    cotangent,
    norm_gain,
    w_gate,
    w_up,
    w_down,
):
    sequence = lax.axis_index(("dp", "expert"))
    ids = prompt_ids[tenant[0]]
    live = (jnp.arange(PROMPT, dtype=jnp.int32) < lengths[0]).astype(F32)
    facts = jnp.concatenate(
        [
            ids[None].astype(F32),
            live[None],
            routes.T.astype(F32),
            route_weight.T * live[None],
            jnp.zeros((2, PROMPT), F32),
        ],
        axis=0,
    )
    facts = lax.dynamic_update_slice(
        jnp.zeros((8, TOKENS), F32), facts, (0, sequence * PROMPT)
    )
    gain = norm_gain.reshape(48, 128)
    vmem = pl.BlockSpec(memory_space=pltpu.VMEM)
    hbm = pl.BlockSpec(memory_space=pl.ANY)
    sums_shape = pltpu.VMEM((4, 4, 4, 4, 16, 384), BF16)
    copies = Slots.COUNT
    return pl.pallas_call(
        kernel,
        out_shape=jax.ShapeDtypeStruct((16, 384), F32),
        in_specs=[vmem] * 4 + [hbm] * 3,
        out_specs=vmem,
        scratch_shapes=[
            pltpu.VMEM((3, 4, 4, 4, 4, POOL_ROWS, 128), BF16),
            pltpu.VMEM((3, 4, 4, 4, 4, COT_ROWS, 128), BF16),
            pltpu.VMEM((48, 128, 256), BF16),
            pltpu.VMEM((128, D), BF16),
            pltpu.VMEM((3, 32, 128), BF16),
            pltpu.VMEM((3, 32, 128), BF16),
            pltpu.VMEM((7, 8, TOKENS), F32),
            pltpu.VMEM((3, 8, TOKENS), F32),
            pltpu.VMEM((512, 256), F32),
            pltpu.VMEM((TOKENS, 128), F32),
            pltpu.VMEM((512, 128), F32),
            pltpu.VMEM((512, 128), F32),
            pltpu.VMEM((2, 256, 256), BF16),
            sums_shape,
            sums_shape,
            sums_shape,
            pltpu.VMEM((4, 3, 4, 2, 16, 384), BF16),
            pltpu.VMEM((4, 3, 4, 2, 16, 384), BF16),
            pltpu.VMEM((4, 4, 2, 16, 384), BF16),
            pltpu.VMEM((4, 4, 2, 16, 384), BF16),
            pltpu.VMEM((4, 3, 2, 16, 384), BF16),
            pltpu.VMEM((4, 3, 2, 16, 384), BF16),
            pltpu.VMEM((4, 4, 16, 384), BF16),
            pltpu.VMEM((16, 16, 384), BF16),
            pltpu.VMEM((8, 512), F32),
            pltpu.VMEM((8, 512), F32),
            pltpu.VMEM((8, 512), F32),
            pltpu.VMEM((4, 8, 128), F32),
            pltpu.VMEM((4, 8, 128), F32),
            pltpu.VMEM((16, 8, 128), F32),
            pltpu.VMEM((48, 128), F32),
            pltpu.SemaphoreType.DMA((3,)),
            pltpu.SemaphoreType.DMA((copies,)),
            pltpu.SemaphoreType.DMA((copies,)),
        ],
        compiler_params=pltpu.CompilerParams(
            collective_id=0, has_side_effects=True, vmem_limit_bytes=56 * 2**20
        ),
        name="moe_backward",
    )(
        pool,
        cotangent,
        facts,
        gain,
        w_gate.reshape(48, 128, 128),
        w_up.reshape(48, 128, 128),
        w_down[0],
    )


def solution(mesh):
    placed = (
        P(("dp", "expert"), "tensor"),
        P(),
        P(("dp", "expert")),
        P(("dp", "expert")),
        P(("dp", "expert"), None),
        P(("dp", "expert"), None),
        P(("dp", "expert"), "tensor"),
        P(),
        P("expert", None, ("dp", "tensor")),
        P("expert", None, ("dp", "tensor")),
        P("expert", ("dp", "tensor"), None),
    )
    return jax.shard_map(
        local, mesh=mesh, in_specs=placed, out_specs=P(("dp", "expert"), "tensor"), check_vma=False
    )
```

```python
import jax
import jax.numpy as jnp
from jax import lax
from jax.experimental import pallas as pl
from jax.experimental.pallas import tpu as pltpu
from jax.sharding import PartitionSpec as P

D = 6144
EPSILON = 1e-05
MESH = pl.DeviceIdType.MESH
F32, BF16 = jnp.float32, jnp.bfloat16
POOL_ROWS, COT_ROWS, PROMPT = 32, 48, 24
TOKENS = 768
GROUP_ORDER = (2, 1, 3, 0)
NT = (((1,), (1,)), ((), ()))
KEEP = slice(None)
NEAR = (1, 15)
TURN, PASS, END, ROUND = 1, 2, 3, 4


class Net:
    def __init__(self, send_sems, recv_sems):
        self.x = lax.axis_index("dp")
        expert = lax.axis_index("expert")
        tensor = lax.axis_index("tensor")
        self.zl, self.c = expert // 2, expert % 2
        self.zh, self.y = tensor // 4, tensor % 4
        self.z = self.zh * 4 + self.zl
        self.send_sems, self.recv_sems = send_sems, recv_sems
        self.slots = {}
        self.sent = {}

    def device(self, x=None, y=None, z=None, c=None):
        x = self.x if x is None else x
        y = self.y if y is None else y
        z = self.z if z is None else z
        c = self.c if c is None else c
        return (x, (z % 4) * 2 + c, (z // 4) * 4 + y)

    def copy(self, key, src, dst, device):
        slot = self.slots.setdefault(key, len(self.slots))
        assert slot < Slots.STATIC
        return self.copy_at(slot, src, dst, device)

    def copy_at(self, slot, src, dst, device):
        return pltpu.make_async_remote_copy(
            src_ref=src,
            dst_ref=dst,
            send_sem=self.send_sems.at[slot],
            recv_sem=self.recv_sems.at[slot],
            device_id=device,
            device_id_type=MESH,
        )

    def start(self, key, src, dst, device):
        copy = self.copy(key, src, dst, device)
        copy.start()
        self.sent[key] = copy

    def wait(self, key, dst):
        self.copy(key, dst, dst, self.device(c=1 - self.c)).wait_recv()

    def drain(self):
        for copy in self.sent.values():
            copy.wait_send()
        self.sent = {}

    def drain_sizes(self, sizes, stand_in):
        for key, shape, dtype in sizes:
            ref = stand_in(shape, dtype)
            self.copy(key, ref, ref, self.device(c=1 - self.c)).wait_send()


def kind(core, o):
    return "cot" if (core + o) % 2 == 0 else "pool"


def spot(o, z, y, x):
    zh, zl = (KEEP, KEEP) if z is None else (z // 4, z % 4)
    return (o, zh, KEEP if y is None else y, KEEP if x is None else x, zl)


def ring_steps(core, size):
    return (size // 2, size // 2 - 1) if core == 0 else (size // 2 - 1, size // 2)


class Slots:
    STATIC = 140
    LINE = STATIC
    PLANE = LINE + 6 * 18
    HAND = PLANE + 2 * 16 * 7
    Z = HAND + 3 * 16
    COUNT = Z + 16

    @staticmethod
    def line(number, sign, step):
        return Slots.LINE + number * 18 + (0 if sign == 1 else 9) + step

    @staticmethod
    def plane(o, distance, which):
        return Slots.PLANE + (o * 16 + distance) * 7 + which

    @staticmethod
    def hand(o, distance):
        return Slots.HAND + o * 16 + distance


class Gather:
    def __init__(self, net, core, bufs):
        self.net, self.core, self.bufs = net, core, bufs
        right, left = ring_steps(core, 16)
        self.signs = ((1, 0, right), (-1, 1, left))
        self.long = 1 if core == 0 else -1

    def unit(self, o, z, y, x):
        return self.bufs[kind(self.core, o)].at[spot(o, z, y, x)]

    def send(self, slot, unit, device):
        self.net.copy_at(slot, unit, unit, device).start()

    def wait(self, slot, unit):
        self.net.copy_at(slot, unit, unit, self.net.device(c=1 - self.net.c)).wait_recv()

    def wait_sent(self, slot, unit):
        self.net.copy_at(slot, unit, unit, self.net.device(c=1 - self.net.c)).wait_send()

    def distance(self, sign, step):
        return (16 - step) % 16 if sign == 1 else step % 16

    def line_unit(self, number, pos):
        net = self.net
        if number < 2:
            return self.unit(number, pos, net.y, net.x)
        return self.unit(2, pos, None, (net.x - (number - 2)) % 4)

    def line_send(self, number, sign, step):
        net = self.net
        unit = self.line_unit(number, (net.z + 16 - sign * (step - 1)) % 16)
        self.send(Slots.line(number, sign, step), unit, net.device(z=(net.z + 16 + sign) % 16))

    def line_step(self, number, sign, count, step):
        unit = self.line_unit(number, (self.net.z + 16 - sign * step) % 16)
        self.wait(Slots.line(number, sign, step), unit)

        @pl.when(step < count)
        def _():
            self.line_send(number, sign, step + 1)

    def one(self, o, z, step):
        net = self.net
        if o == 0:
            return self.unit(o, z, (net.y + step) % 4, net.x)
        return self.unit(o, z, net.y, (net.x + step) % 4)

    def two(self, o, z, step):
        net = self.net
        if o == 0:
            return self.unit(o, z, None, (net.x + step) % 4)
        return self.unit(o, z, (net.y + step) % 4, None)

    def along(self, o, ring, step):
        net = self.net
        if (o == 0) == (ring == 0):
            return net.device(y=(net.y + step) % 4)
        return net.device(x=(net.x + step) % 4)

    def plane_start(self, o, sign, step):
        d = self.distance(sign, step)
        z = (self.net.z + d) % 16
        for j in (2, 1, 3):
            self.send(Slots.plane(o, d, j - 1), self.one(o, z, 0), self.along(o, 0, j))

    def plane_turn(self, o, sign, step):
        d = self.distance(sign, step)
        z = (self.net.z + d) % 16
        for j in (1, 3, 2):
            self.wait(Slots.plane(o, d, j - 1), self.one(o, z, 4 - j))
        for slot, way in ((3, self.long), (4, -self.long)):
            self.send(Slots.plane(o, d, slot), self.two(o, z, 0), self.along(o, 1, 4 + way))

    def plane_pass(self, o, sign, step):
        d = self.distance(sign, step)
        z = (self.net.z + d) % 16
        self.wait(Slots.plane(o, d, 3), self.two(o, z, 4 - self.long))
        self.send(
            Slots.plane(o, d, 5), self.two(o, z, 4 - self.long), self.along(o, 1, 4 + self.long)
        )
        self.wait(Slots.plane(o, d, 4), self.two(o, z, 4 + self.long))

    def plane_end(self, o, sign, step):
        d = self.distance(sign, step)
        z = (self.net.z + d) % 16
        self.wait(Slots.plane(o, d, 5), self.two(o, z, 2))
        self.hand_over(o, d)

    def hand_over(self, o, d):
        net = self.net
        unit = self.unit(o, (net.z + d) % 16, None, None)
        self.send(Slots.hand(o, d), unit, net.device(c=1 - net.c))

    def begin(self):
        net = self.net
        for number in (0, 1):
            self.line_send(number, 1, 1)
            self.line_send(number, -1, 1)
        own = self.unit(2, net.z, net.y, net.x)
        for j in (2, 1, 3):
            net.start(("y", j), own, own, net.device(y=(net.y + j) % 4))

    def own_line(self):
        net = self.net
        for j in (1, 3, 2):
            net.wait(("y", j), self.unit(2, net.z, (net.y + 4 - j) % 4, net.x))
        self.line_send(2, 1, 1)
        self.line_send(2, -1, 1)
        own = self.unit(2, net.z, None, net.x)
        for j in (2, 1, 3):
            net.start(("x", j), own, own, net.device(x=(net.x + j) % 4))

    def other_lines(self):
        net = self.net
        for j in (1, 3, 2):
            net.wait(("x", j), self.unit(2, net.z, None, (net.x + 4 - j) % 4))
            self.line_send(2 + j, 1, 1)
            self.line_send(2 + j, -1, 1)
        self.hand_over(2, 0)

    def steps(self, s, facts):
        for sign, first, count in self.signs:

            @pl.when((s >= 1) & (s <= count))
            def _():
                self.line_step(0, sign, count, s)
                self.line_step(1, sign, count, s)

            @pl.when((s >= first) & (s <= count))
            def _():
                self.plane_start(0, sign, s)
                self.plane_start(1, sign, s)

        pl.when(s == 1)(self.own_line)
        pl.when(s == 2)(self.other_lines)
        for sign, first, count in self.signs:

            @pl.when((s >= ROUND + 1) & (s - ROUND <= count))
            def _():
                for number in range(2, 6):
                    self.line_step(number, sign, count, s - ROUND)
                self.hand_over(2, self.distance(sign, s - ROUND))

        for late, stage in ((TURN, self.plane_turn), (PASS, self.plane_pass), (END, self.plane_end)):
            for sign, first, count in self.signs:

                @pl.when((s >= late + first) & (s - late <= count))
                def _():
                    stage(0, sign, s - late)
                    stage(1, sign, s - late)

        for number, stage in enumerate(facts):
            pl.when(s == 2 + 2 * number)(stage)

    def run(self, facts):
        def body(s, carry):
            self.steps(s, facts)
            return carry

        self.begin()
        lax.fori_loop(0, max(END, ROUND) + 9, body, 0)

    def landed(self, o):
        other = self.bufs[kind(1 - self.core, o)]

        def body(d, carry):
            self.wait(Slots.hand(o, d), other.at[spot(o, (self.net.z + d) % 16, None, None)])
            return carry

        lax.fori_loop(0, 16, body, 0)

    def drain(self):
        def blocks(d, carry):
            for o in (0, 1):
                for which in range(3):
                    self.wait_sent(Slots.plane(o, d, which), self.unit(o, 0, 0, 0))
                for which in range(3, 6):
                    self.wait_sent(Slots.plane(o, d, which), self.unit(o, 0, None, 0))
            for o in range(3):
                self.wait_sent(Slots.hand(o, d), self.unit(o, 0, None, None))
            return carry

        lax.fori_loop(0, 16, blocks, 0)
        for sign, _, count in self.signs:

            def lines(step, carry, sign=sign):
                for number in range(6):
                    unit = self.unit(min(number, 2), 0, 0 if number < 2 else None, 0)
                    self.wait_sent(Slots.line(number, sign, step), unit)
                return carry

            lax.fori_loop(1, count + 1, lines, 0)


def facts_stages(net, facts_ref, facts_got, facts_sum):
    net.start(("facts", 0), facts_ref, facts_got.at[0], net.device(c=1 - net.c))

    def pair():
        net.wait(("facts", 0), facts_got.at[0])
        facts_sum[0] = facts_ref[...] + facts_got[0]
        for j in (1, 2, 3):
            there = net.device(z=net.zh * 4 + (net.zl + j) % 4)
            net.start(("facts", j), facts_sum.at[0], facts_got.at[j], there)

    def near():
        for j in (1, 2, 3):
            net.wait(("facts", j), facts_got.at[j])
        facts_sum[1] = facts_sum[0] + facts_got[1] + facts_got[2] + facts_got[3]
        for j in (1, 2, 3):
            there = net.device(x=(net.x + j) % 4)
            net.start(("facts", 3 + j), facts_sum.at[1], facts_got.at[3 + j], there)

    def whole():
        for j in (1, 2, 3):
            net.wait(("facts", 3 + j), facts_got.at[3 + j])
        facts_sum[2] = facts_sum[1] + facts_got[4] + facts_got[5] + facts_got[6]

    return pair, near, whole


def gather(net, core, pool_ref, cot_ref, facts_ref, bufs, padded, landed, facts_got, facts_sum):
    partner = net.device(c=1 - net.c)
    here = (net.zh, net.y, net.x, net.zl)
    own_rows = pl.ds(16 * core, 16)
    for o in range(3):
        columns = slice(o * 128, (o + 1) * 128)
        if kind(core, o) == "cot":
            dst = bufs["pool"].at[(o,) + here + (own_rows,)]
            net.start(("swap", o), pool_ref.at[:, pl.ds(o * 128, 128)], dst, partner)
        else:
            block = cot_ref[:, columns].astype(F32)
            padded[o] = jnp.concatenate([block, jnp.zeros((8, 128), F32)], axis=0).astype(BF16)
            net.start(("swap", o), padded.at[o], landed.at[o], partner)
    for o in range(3):
        columns = slice(o * 128, (o + 1) * 128)
        if kind(core, o) == "pool":
            bufs["pool"][(o,) + here + (own_rows,)] = pool_ref[:, columns]
            net.wait(("swap", o), bufs["pool"].at[(o,) + here + (pl.ds(16 * (1 - core), 16),)])
        else:
            net.wait(("swap", o), landed.at[o])
            own = cot_ref[:, columns].astype(F32)
            other = landed[o].astype(F32)[:PROMPT]
            pair = [own, other] if core == 0 else [other, own]
            bufs["cot"][(o,) + here] = jnp.concatenate(pair, axis=0).astype(BF16)
    work = Gather(net, core, bufs)
    work.run(facts_stages(net, facts_ref, facts_got, facts_sum))
    return [(key, copy.src_ref.shape, copy.src_ref.dtype) for key, copy in net.sent.items()]


def build_facts(net, ids_ref, tenant_ref, lengths_ref, routes_ref, route_weight_ref, facts_ref):
    sequence = (net.x * 4 + net.zl) * 2 + net.c
    row = lax.broadcasted_iota(jnp.int32, (PROMPT, TOKENS), 0) + sequence * PROMPT
    place = jnp.where(lax.broadcasted_iota(jnp.int32, (PROMPT, TOKENS), 1) == row, 1.0, 0.0)
    ids = jnp.broadcast_to(ids_ref[pl.ds(tenant_ref[0], 1), :].astype(F32), (8, PROMPT))
    spread = jnp.dot(
        ids, place, precision=lax.Precision.HIGHEST, preferred_element_type=F32
    )
    facts_ref[...] = jnp.zeros_like(facts_ref)
    facts_ref[0:1] = spread[0:1]
    live = place * jnp.where(
        lax.broadcasted_iota(jnp.int32, (PROMPT, TOKENS), 0) < lengths_ref[0], 1.0, 0.0
    )
    facts_ref[1:2] = jnp.sum(live, axis=0, keepdims=True)
    for k in range(2):
        route = routes_ref[:, k : k + 1].astype(F32)
        facts_ref[2 + k : 3 + k] = jnp.sum(place * route, axis=0, keepdims=True)
        weight = route_weight_ref[:, k : k + 1]
        facts_ref[4 + k : 5 + k] = jnp.sum(live * weight, axis=0, keepdims=True)


def kernel(
    pool_ref,
    cot_ref,
    ids_ref,
    tenant_ref,
    lengths_ref,
    routes_ref,
    route_weight_ref,
    gain_ref,
    w_gate_hbm,
    w_up_hbm,
    w_down_hbm,
    out_ref,
    pool_buf,
    cot_buf,
    w_in,
    w_out,
    padded,
    landed,
    facts_got,
    facts_sum,
    hidden,
    back,
    squares,
    scales,
    grads,
    part_out,
    part_in,
    sums,
    first_a,
    first_b,
    mid_a,
    mid_b,
    second_a,
    second_b,
    plane,
    last,
    dot_own,
    dot_pair,
    dot_sum,
    dot_x,
    dot_y,
    dot_z,
    gain_all,
    facts_ref,
    weight_sems,
    send_sems,
    recv_sems,
):
    gain_all[...] = gain_ref[...].astype(F32)
    net = Net(send_sems, recv_sems)
    partner = net.device(c=1 - net.c)
    loads = [
        pltpu.make_async_copy(w_gate_hbm, w_in.at[:, :, pl.ds(0, 128)], weight_sems.at[0]),
        pltpu.make_async_copy(w_up_hbm, w_in.at[:, :, pl.ds(128, 128)], weight_sems.at[1]),
        pltpu.make_async_copy(w_down_hbm, w_out, weight_sems.at[2]),
    ]
    for load in loads:
        load.start()

    build_facts(net, ids_ref, tenant_ref, lengths_ref, routes_ref, route_weight_ref, facts_ref)
    barrier = pltpu.get_barrier_semaphore()
    peers = [partner]
    for j in (1, 2, 3):
        peers += [net.device(x=(net.x + j) % 4), net.device(y=(net.y + j) % 4)]
    peers += [net.device(z=(net.z + j) % 16) for j in NEAR]
    for peer in peers:
        pl.semaphore_signal(barrier, inc=1, device_id=peer, device_id_type=MESH)
    pl.semaphore_wait(barrier, len(peers))

    bufs = {"pool": pool_buf, "cot": cot_buf}
    sizes = [None, None]
    for core in range(2):

        @pl.when(net.c == core)
        def _():
            branch = Net(send_sems, recv_sems)
            branch.slots = net.slots
            sizes[core] = gather(
                branch, core, pool_ref, cot_ref, facts_ref, bufs, padded, landed, facts_got, facts_sum
            )

    for load in loads:
        load.wait()

    def stand_in(shape, dtype):
        if dtype == F32:
            return facts_sum.at[0]
        if shape == (16, 128):
            return padded.at[0, pl.ds(0, 16)]
        if shape == (32, 128):
            return padded.at[0]
        buf = pool_buf if shape[-2] == POOL_ROWS else cot_buf
        ref = buf.at[(0,) * (7 - len(shape))]
        assert ref.shape == shape
        return ref

    def drain_gather():
        for core in range(2):

            @pl.when(net.c == core)
            def _():
                net.drain_sizes(sizes[core], stand_in)
                Gather(net, core, bufs).drain()

    hidden[...] = jnp.zeros_like(hidden)
    back[...] = jnp.zeros_like(back)
    squares[...] = jnp.zeros_like(squares)
    for o in range(3):

        def columns_step(zh, carry, o=o):
            blocks = [(zh * 4 + y) * 3 + o for y in range(4)]
            normed = []
            square = None
            for y in range(4):
                value = pool_buf[o, zh, y].reshape(16 * POOL_ROWS, 128).astype(F32)
                square = value * value if square is None else square + value * value
                normed.append((value * gain_all[pl.ds(blocks[y], 1), :]).astype(BF16))
            squares[...] += square
            weights = jnp.concatenate([w_in[b] for b in blocks], axis=0)
            hidden[...] += jnp.dot(
                jnp.concatenate(normed, axis=1), weights, preferred_element_type=F32
            )
            cots = jnp.concatenate(
                [cot_buf[o, zh, y].reshape(TOKENS, 128) for y in range(4)], axis=1
            )
            downs = jnp.concatenate(
                [w_out[:, pl.ds(pl.multiple_of(b * 128, 128), 128)] for b in blocks], axis=1
            )
            back[...] += lax.dot_general(cots, downs, NT, preferred_element_type=F32)
            return carry

        for core in range(2):

            @pl.when(net.c == core)
            def _():
                Gather(net, core, bufs).landed(o)

        lax.fori_loop(0, 4, columns_step, 0)

    ids = facts_sum[2, 0:1]
    live = facts_sum[2, 1:2]
    expert = (net.zl * 2 + net.c).astype(F32)
    weight = jnp.where(facts_sum[2, 2:3] == expert, facts_sum[2, 4:5], 0.0) + jnp.where(
        facts_sum[2, 3:4] == expert, facts_sum[2, 5:6], 0.0
    )
    back_all = back[...]
    back_hi = back_all.astype(BF16)
    back_lo = (back_all - back_hi.astype(F32)).astype(BF16)

    def rows_step(i, carry):
        rows = pl.ds(pl.multiple_of(i * 128, 128), 128)
        number = (lax.broadcasted_iota(jnp.int32, (128, 1), 0) + i * 128).astype(F32)
        place = jnp.where(ids == number, weight, 0.0)
        place_hi = place.astype(BF16)
        place_lo = (place - place_hi.astype(F32)).astype(BF16)
        got = jnp.dot(place_hi, back_hi, preferred_element_type=F32)
        got += jnp.dot(place_hi, back_lo, preferred_element_type=F32)
        got += jnp.dot(place_lo, back_hi, preferred_element_type=F32)
        scale = lax.rsqrt(jnp.sum(squares[rows], axis=1, keepdims=True) / D + EPSILON)
        scales[rows] = jnp.broadcast_to(scale, (128, 128))
        raw_gate, raw_up = hidden[rows, 0:128], hidden[rows, 128:256]
        gate, up = raw_gate * scale, raw_up * scale
        sigma = jax.nn.sigmoid(gate)
        grad_gate = got * up * sigma * (1.0 + gate * (1.0 - sigma))
        grad_up = got * (gate * sigma)
        both = jnp.concatenate([grad_gate, grad_up], axis=1).astype(BF16).reshape(4, 2, 16, 256)
        half = pl.ds(pl.multiple_of(i * 64, 64), 64)
        grads[0, half] = both[:, 0].reshape(64, 256)
        grads[1, half] = both[:, 1].reshape(64, 256)
        product = grad_gate * raw_gate + grad_up * raw_up
        dot_own[:, rows] = lax.dot_general(
            jnp.ones((8, 128), F32),
            product,
            NT,
            precision=lax.Precision.HIGHEST,
            preferred_element_type=F32,
        )
        return carry

    lax.fori_loop(0, 4, rows_step, 0)

    def product(parity, zh, y):
        weights = jnp.concatenate([w_in[(zh * 4 + y) * 3 + o] for o in range(3)], axis=0)
        return lax.dot_general(grads[parity], weights, NT, preferred_element_type=F32)

    net.start("dot_pair", dot_own, dot_pair, partner)
    spots = [(net.zh + step) % 4 for step in GROUP_ORDER]

    def other(g):
        zh = spots[g]

        def other_step(y, carry):
            part_out[zh, y] = product(1 - net.c, zh, y).astype(BF16).reshape(4, 4, 16, 384)
            return carry

        lax.fori_loop(0, 4, other_step, 0)
        net.start(("part", g), part_out.at[zh], part_in.at[zh], partner)

    lanes = [pl.ds(pl.multiple_of((net.x + j) % 4 * 128, 128), 128) for j in range(4)]

    def begin(g):
        zh = spots[g]
        net.wait(("part", g), part_in.at[zh])

        def own_step(y, carry):
            total = product(net.c, zh, y).reshape(4, 4, 16, 384) + part_in[zh, y].astype(F32)
            sums[zh, y] = total.astype(BF16)
            return carry

        lax.fori_loop(0, 4, own_step, 0)
        for h in range(2):
            for j in (2, 1, 3):
                x, y = (net.x + j) % 4, (net.y + j) % 4
                to_x, to_y = net.device(x=x), net.device(y=y)
                net.start(("a1", g, h, j), sums.at[zh, :, x, h], first_a.at[g, h, j - 1], to_x)
                net.start(("b1", g, h, j), sums.at[zh, y, :, 2 + h], first_b.at[g, h, j - 1], to_y)

    def middle(g, h):
        zh = spots[g]
        for j in (1, 2, 3):
            net.wait(("a1", g, h, j), first_a.at[g, h, j - 1])
            net.wait(("b1", g, h, j), first_b.at[g, h, j - 1])
        own_a = sums[zh, :, net.x, h].astype(F32)
        own_b = sums[zh, net.y, :, 2 + h].astype(F32)
        for j in range(3):
            own_a += first_a[g, h, j].astype(F32)
            own_b += first_b[g, h, j].astype(F32)
        mid_a[g, h] = own_a.astype(BF16)
        mid_b[g, h] = own_b.astype(BF16)
        for j in (2, 1, 3):
            x, y = (net.x + j) % 4, (net.y + j) % 4
            to_x, to_y = net.device(x=x), net.device(y=y)
            net.start(("a2", g, h, j), mid_a.at[g, h, y], second_a.at[g, h, j - 1], to_y)
            net.start(("b2", g, h, j), mid_b.at[g, h, x], second_b.at[g, h, j - 1], to_x)

    def line_copy(g, zl):
        slot = GROUP_ORDER[g] * 4 + (zl + 4 - net.zl) % 4
        there = net.device(z=spots[g] * 4 + zl)
        return net.copy_at(Slots.Z + slot, plane.at[g, zl], last.at[slot], there)

    def finish(g, h):
        for j in (1, 2, 3):
            net.wait(("a2", g, h, j), second_a.at[g, h, j - 1])
            net.wait(("b2", g, h, j), second_b.at[g, h, j - 1])
        own_a = mid_a[g, h, net.y].astype(F32)
        own_b = mid_b[g, h, net.x].astype(F32)
        for j in range(3):
            own_a += second_a[g, h, j].astype(F32)
            own_b += second_b[g, h, j].astype(F32)
        plane[g, h] = own_a.astype(BF16)
        plane[g, 2 + h] = own_b.astype(BF16)
        for zl in (h, 2 + h):
            if GROUP_ORDER[g] > 0:
                line_copy(g, zl).start()
            else:
                pl.when(net.zl != zl)(lambda zl=zl: line_copy(g, zl).start())

    def dot_one():
        net.wait("dot_pair", dot_pair)
        dot_sum[...] = dot_own[...] + dot_pair[...]
        for j in (1, 2, 3):
            net.start(
                ("dot_x", j), dot_sum.at[:, lanes[j]], dot_x.at[j], net.device(x=(net.x + j) % 4)
            )

    def dot_two():
        for j in (1, 2, 3):
            net.wait(("dot_x", j), dot_x.at[j])
        dot_y[0] = dot_sum[:, lanes[0]] + dot_x[1] + dot_x[2] + dot_x[3]
        for j in (1, 2, 3):
            net.start(("dot_y", j), dot_y.at[0], dot_y.at[j], net.device(y=(net.y + j) % 4))

    def dot_three():
        for j in (1, 2, 3):
            net.wait(("dot_y", j), dot_y.at[j])
        dot_z[0] = dot_y[0] + dot_y[1] + dot_y[2] + dot_y[3]
        for j in range(1, 16):
            net.start(("dot_z", j), dot_z.at[0], dot_z.at[j], net.device(z=(net.z + j) % 16))

    other(0)
    other(1)
    begin(0)
    dot_one()
    other(2)
    begin(1)
    dot_two()
    middle(0, 0)
    middle(0, 1)
    other(3)
    begin(2)
    dot_three()
    middle(1, 0)
    finish(0, 0)
    middle(1, 1)
    finish(0, 1)
    begin(3)
    drain_gather()
    middle(2, 0)
    finish(1, 0)
    middle(2, 1)
    finish(1, 1)

    first = ((net.x * 4 + net.zl) * 2 + net.c) * 16
    own_number = (lax.broadcasted_iota(jnp.int32, (16, 1), 0) + first).astype(F32)
    own_place = jnp.where(ids == own_number, live, 0.0).astype(BF16)
    direct = jnp.concatenate(
        [
            jnp.dot(
                own_place,
                cot_buf[o, net.zh, net.y].reshape(TOKENS, 128),
                preferred_element_type=F32,
            )
            for o in range(3)
        ],
        axis=1,
    )

    middle(3, 0)
    finish(2, 0)
    middle(3, 1)
    finish(2, 1)
    finish(3, 0)
    finish(3, 1)
    net.drain()

    for j in range(1, 16):
        net.wait(("dot_z", j), dot_z.at[j])
    dots = dot_z[0]
    for j in range(1, 16):
        dots += dot_z[j]
    own_lane = (net.zl * 2 + net.c) * 16 + lax.broadcasted_iota(jnp.int32, (16, 128), 0)
    picked = jnp.where(lax.broadcasted_iota(jnp.int32, (16, 128), 1) == own_lane, dots[0:1], 0.0)
    own_dot = jnp.sum(picked, axis=1, keepdims=True)
    scale = scales[pl.ds(pl.multiple_of(first, 16), 16), 0:1]
    factor = scale * scale * scale * own_dot / D

    tile = (net.zh * 4 + net.y) * 3
    own_gain = jnp.concatenate([gain_all[pl.ds(tile + o, 1), :] for o in range(3)], axis=1)
    total = plane[3, net.zl].astype(F32)
    for step in GROUP_ORDER:
        for j in range(4):
            slot = step * 4 + j
            if slot > 0:
                arrival = last.at[slot]
                net.copy_at(Slots.Z + slot, arrival, arrival, partner).wait_recv()
                total += last[slot].astype(F32)
    out_ref[...] = (
        direct + scale * own_gain * total - pool_ref[...].astype(F32) * factor
    )
    for slot in range(1, 16):
        net.copy_at(Slots.Z + slot, plane.at[0, 0], last.at[slot], partner).wait_send()


def local(
    pool,
    prompt_ids,
    tenant,
    lengths,
    routes,
    route_weight,
    cotangent,
    norm_gain,
    w_gate,
    w_up,
    w_down,
):
    gain = norm_gain.reshape(48, 128)
    vmem = pl.BlockSpec(memory_space=pltpu.VMEM)
    hbm = pl.BlockSpec(memory_space=pl.ANY)
    smem = pl.BlockSpec(memory_space=pltpu.SMEM)
    sums_shape = pltpu.VMEM((4, 4, 4, 4, 16, 384), BF16)
    copies = Slots.COUNT
    return pl.pallas_call(
        kernel,
        out_shape=jax.ShapeDtypeStruct((16, 384), F32),
        in_specs=[vmem] * 3 + [smem] * 2 + [vmem] * 3 + [hbm] * 3,
        out_specs=vmem,
        scratch_shapes=[
            pltpu.VMEM((3, 4, 4, 4, 4, POOL_ROWS, 128), BF16),
            pltpu.VMEM((3, 4, 4, 4, 4, COT_ROWS, 128), BF16),
            pltpu.VMEM((48, 128, 256), BF16),
            pltpu.VMEM((128, D), BF16),
            pltpu.VMEM((3, 32, 128), BF16),
            pltpu.VMEM((3, 32, 128), BF16),
            pltpu.VMEM((7, 8, TOKENS), F32),
            pltpu.VMEM((3, 8, TOKENS), F32),
            pltpu.VMEM((512, 256), F32),
            pltpu.VMEM((TOKENS, 128), F32),
            pltpu.VMEM((512, 128), F32),
            pltpu.VMEM((512, 128), F32),
            pltpu.VMEM((2, 256, 256), BF16),
            sums_shape,
            sums_shape,
            sums_shape,
            pltpu.VMEM((4, 2, 3, 4, 16, 384), BF16),
            pltpu.VMEM((4, 2, 3, 4, 16, 384), BF16),
            pltpu.VMEM((4, 2, 4, 16, 384), BF16),
            pltpu.VMEM((4, 2, 4, 16, 384), BF16),
            pltpu.VMEM((4, 2, 3, 16, 384), BF16),
            pltpu.VMEM((4, 2, 3, 16, 384), BF16),
            pltpu.VMEM((4, 4, 16, 384), BF16),
            pltpu.VMEM((16, 16, 384), BF16),
            pltpu.VMEM((8, 512), F32),
            pltpu.VMEM((8, 512), F32),
            pltpu.VMEM((8, 512), F32),
            pltpu.VMEM((4, 8, 128), F32),
            pltpu.VMEM((4, 8, 128), F32),
            pltpu.VMEM((16, 8, 128), F32),
            pltpu.VMEM((48, 128), F32),
            pltpu.VMEM((8, TOKENS), F32),
            pltpu.SemaphoreType.DMA((3,)),
            pltpu.SemaphoreType.DMA((copies,)),
            pltpu.SemaphoreType.DMA((copies,)),
        ],
        compiler_params=pltpu.CompilerParams(
            collective_id=0, has_side_effects=True, vmem_limit_bytes=56 * 2**20
        ),
        name="moe_backward",
    )(
        pool,
        cotangent,
        prompt_ids,
        tenant,
        lengths,
        routes,
        route_weight,
        gain,
        w_gate.reshape(48, 128, 128),
        w_up.reshape(48, 128, 128),
        w_down[0],
    )


def solution(mesh):
    placed = (
        P(("dp", "expert"), "tensor"),
        P(),
        P(("dp", "expert")),
        P(("dp", "expert")),
        P(("dp", "expert"), None),
        P(("dp", "expert"), None),
        P(("dp", "expert"), "tensor"),
        P(),
        P("expert", None, ("dp", "tensor")),
        P("expert", None, ("dp", "tensor")),
        P("expert", ("dp", "tensor"), None),
    )
    return jax.shard_map(
        local, mesh=mesh, in_specs=placed, out_specs=P(("dp", "expert"), "tensor"), check_vma=False
    )
```

```python
import jax
import jax.numpy as jnp
from jax import lax
from jax.experimental import pallas as pl
from jax.experimental.pallas import tpu as pltpu
from jax.sharding import PartitionSpec as P

D = 6144
EPSILON = 1e-05
MESH = pl.DeviceIdType.MESH
F32, BF16 = jnp.float32, jnp.bfloat16
POOL_ROWS, COT_ROWS, PROMPT = 32, 48, 24
TOKENS = 768
GROUP_ORDER = (2, 1, 3, 0)
NT = (((1,), (1,)), ((), ()))
KEEP = slice(None)
NEAR = (1, 15)
TURN, PASS, END, ROUND = 1, 2, 3, 4


def mod(value, size):
    return value % size if isinstance(value, int) else lax.rem(value, size)


def div(value, size):
    return value // size if isinstance(value, int) else lax.div(value, size)


class Net:
    def __init__(self, send_sems, recv_sems):
        self.x = lax.axis_index("dp")
        expert = lax.axis_index("expert")
        tensor = lax.axis_index("tensor")
        self.zl, self.c = div(expert, 2), mod(expert, 2)
        self.zh, self.y = div(tensor, 4), mod(tensor, 4)
        self.z = self.zh * 4 + self.zl
        self.send_sems, self.recv_sems = send_sems, recv_sems
        self.slots = {}
        self.sent = {}

    def device(self, x=None, y=None, z=None, c=None):
        x = self.x if x is None else x
        y = self.y if y is None else y
        z = self.z if z is None else z
        c = self.c if c is None else c
        return (x, (mod(z, 4)) * 2 + c, (div(z, 4)) * 4 + y)

    def copy(self, key, src, dst, device):
        slot = self.slots.setdefault(key, len(self.slots))
        assert slot < Slots.STATIC
        return self.copy_at(slot, src, dst, device)

    def copy_at(self, slot, src, dst, device):
        return pltpu.make_async_remote_copy(
            src_ref=src,
            dst_ref=dst,
            send_sem=self.send_sems.at[slot],
            recv_sem=self.recv_sems.at[slot],
            device_id=device,
            device_id_type=MESH,
        )

    def start(self, key, src, dst, device):
        copy = self.copy(key, src, dst, device)
        copy.start()
        self.sent[key] = copy

    def wait(self, key, dst):
        self.copy(key, dst, dst, self.device(c=1 - self.c)).wait_recv()

    def drain(self):
        for copy in self.sent.values():
            copy.wait_send()
        self.sent = {}

    def drain_sizes(self, sizes, stand_in):
        for key, shape, dtype in sizes:
            ref = stand_in(shape, dtype)
            self.copy(key, ref, ref, self.device(c=1 - self.c)).wait_send()


def kind(core, o):
    return "cot" if mod(core + o, 2) == 0 else "pool"


def spot(o, z, y, x):
    zh, zl = (KEEP, KEEP) if z is None else (div(z, 4), mod(z, 4))
    return (o, zh, KEEP if y is None else y, KEEP if x is None else x, zl)


def ring_steps(core, size):
    return (div(size, 2), div(size, 2) - 1) if core == 0 else (div(size, 2) - 1, div(size, 2))


class Slots:
    STATIC = 140
    LINE = STATIC
    PLANE = LINE + 6 * 18
    HAND = PLANE + 2 * 16 * 7
    Z = HAND + 3 * 16
    COUNT = Z + 16

    @staticmethod
    def line(number, sign, step):
        return Slots.LINE + number * 18 + (0 if sign == 1 else 9) + step

    @staticmethod
    def plane(o, distance, which):
        return Slots.PLANE + (o * 16 + distance) * 7 + which

    @staticmethod
    def hand(o, distance):
        return Slots.HAND + o * 16 + distance


class Gather:
    def __init__(self, net, core, bufs):
        self.net, self.core, self.bufs = net, core, bufs
        right, left = ring_steps(core, 16)
        self.signs = ((1, 0, right), (-1, 1, left))
        self.long = 1 if core == 0 else -1

    def unit(self, o, z, y, x):
        return self.bufs[kind(self.core, o)].at[spot(o, z, y, x)]

    def send(self, slot, unit, device):
        self.net.copy_at(slot, unit, unit, device).start()

    def wait(self, slot, unit):
        self.net.copy_at(slot, unit, unit, self.net.device(c=1 - self.net.c)).wait_recv()

    def wait_sent(self, slot, unit):
        self.net.copy_at(slot, unit, unit, self.net.device(c=1 - self.net.c)).wait_send()

    def distance(self, sign, step):
        return mod(16 - step, 16) if sign == 1 else mod(step, 16)

    def line_unit(self, number, pos):
        net = self.net
        if number < 2:
            return self.unit(number, pos, net.y, net.x)
        return self.unit(2, pos, None, mod(net.x + 6 - number, 4))

    def line_send(self, number, sign, step):
        net = self.net
        unit = self.line_unit(number, mod(net.z + 16 - sign * (step - 1), 16))
        self.send(Slots.line(number, sign, step), unit, net.device(z=mod(net.z + 16 + sign, 16)))

    def line_step(self, number, sign, count, step):
        unit = self.line_unit(number, mod(self.net.z + 16 - sign * step, 16))
        self.wait(Slots.line(number, sign, step), unit)

        @pl.when(step < count)
        def _():
            self.line_send(number, sign, step + 1)

    def one(self, o, z, step):
        net = self.net
        if o == 0:
            return self.unit(o, z, mod(net.y + step, 4), net.x)
        return self.unit(o, z, net.y, mod(net.x + step, 4))

    def two(self, o, z, step):
        net = self.net
        if o == 0:
            return self.unit(o, z, None, mod(net.x + step, 4))
        return self.unit(o, z, mod(net.y + step, 4), None)

    def along(self, o, ring, step):
        net = self.net
        if (o == 0) == (ring == 0):
            return net.device(y=mod(net.y + step, 4))
        return net.device(x=mod(net.x + step, 4))

    def plane_start(self, o, sign, step):
        d = self.distance(sign, step)
        z = mod(self.net.z + d, 16)
        for j in (2, 1, 3):
            self.send(Slots.plane(o, d, j - 1), self.one(o, z, 0), self.along(o, 0, j))

    def plane_turn(self, o, sign, step):
        d = self.distance(sign, step)
        z = mod(self.net.z + d, 16)
        for j in (1, 3, 2):
            self.wait(Slots.plane(o, d, j - 1), self.one(o, z, 4 - j))
        for slot, way in ((3, self.long), (4, -self.long)):
            self.send(Slots.plane(o, d, slot), self.two(o, z, 0), self.along(o, 1, 4 + way))

    def plane_pass(self, o, sign, step):
        d = self.distance(sign, step)
        z = mod(self.net.z + d, 16)
        self.wait(Slots.plane(o, d, 3), self.two(o, z, 4 - self.long))
        self.send(
            Slots.plane(o, d, 5), self.two(o, z, 4 - self.long), self.along(o, 1, 4 + self.long)
        )
        self.wait(Slots.plane(o, d, 4), self.two(o, z, 4 + self.long))

    def plane_end(self, o, sign, step):
        d = self.distance(sign, step)
        z = mod(self.net.z + d, 16)
        self.wait(Slots.plane(o, d, 5), self.two(o, z, 2))
        self.hand_over(o, d)

    def hand_over(self, o, d):
        net = self.net
        unit = self.unit(o, mod(net.z + d, 16), None, None)
        self.send(Slots.hand(o, d), unit, net.device(c=1 - net.c))

    def begin(self):
        net = self.net
        for number in (0, 1):
            self.line_send(number, 1, 1)
            self.line_send(number, -1, 1)
        own = self.unit(2, net.z, net.y, net.x)
        for j in (2, 1, 3):
            net.start(("y", j), own, own, net.device(y=mod(net.y + j, 4)))

    def own_line(self):
        net = self.net
        for j in (1, 3, 2):
            net.wait(("y", j), self.unit(2, net.z, mod(net.y + 4 - j, 4), net.x))
        self.line_send(2, 1, 1)
        self.line_send(2, -1, 1)
        own = self.unit(2, net.z, None, net.x)
        for j in (2, 1, 3):
            net.start(("x", j), own, own, net.device(x=mod(net.x + j, 4)))

    def other_lines(self):
        net = self.net
        for j in (1, 3, 2):
            net.wait(("x", j), self.unit(2, net.z, None, mod(net.x + 4 - j, 4)))
            self.line_send(2 + j, 1, 1)
            self.line_send(2 + j, -1, 1)
        self.hand_over(2, 0)

    def steps(self, s, facts):
        for sign, first, count in self.signs:

            @pl.when((s >= 1) & (s <= count))
            def _():
                self.line_step(0, sign, count, s)
                self.line_step(1, sign, count, s)

            @pl.when((s >= first) & (s <= count))
            def _():
                self.plane_start(0, sign, s)
                self.plane_start(1, sign, s)

        pl.when(s == 1)(self.own_line)
        pl.when(s == 2)(self.other_lines)
        for sign, first, count in self.signs:

            @pl.when((s >= ROUND + 1) & (s - ROUND <= count))
            def _():
                for number in range(2, 6):
                    self.line_step(number, sign, count, s - ROUND)
                self.hand_over(2, self.distance(sign, s - ROUND))

        for late, stage in ((TURN, self.plane_turn), (PASS, self.plane_pass), (END, self.plane_end)):
            for sign, first, count in self.signs:

                @pl.when((s >= late + first) & (s - late <= count))
                def _():
                    stage(0, sign, s - late)
                    stage(1, sign, s - late)

        for number, stage in enumerate(facts):
            pl.when(s == 2 + 2 * number)(stage)

    def run(self, facts):
        def body(s, carry):
            self.steps(s, facts)
            return carry

        self.begin()
        lax.fori_loop(0, max(END, ROUND) + 9, body, 0)

    def landed(self, o):
        other = self.bufs[kind(1 - self.core, o)]

        def body(d, carry):
            self.wait(Slots.hand(o, d), other.at[spot(o, mod(self.net.z + d, 16), None, None)])
            return carry

        lax.fori_loop(0, 16, body, 0)

    def drain(self):
        def blocks(d, carry):
            for o in (0, 1):
                for which in range(3):
                    self.wait_sent(Slots.plane(o, d, which), self.unit(o, 0, 0, 0))
                for which in range(3, 6):
                    self.wait_sent(Slots.plane(o, d, which), self.unit(o, 0, None, 0))
            for o in range(3):
                self.wait_sent(Slots.hand(o, d), self.unit(o, 0, None, None))
            return carry

        lax.fori_loop(0, 16, blocks, 0)
        for sign, _, count in self.signs:

            def lines(step, carry, sign=sign):
                for number in range(6):
                    unit = self.unit(min(number, 2), 0, 0 if number < 2 else None, 0)
                    self.wait_sent(Slots.line(number, sign, step), unit)
                return carry

            lax.fori_loop(1, count + 1, lines, 0)


def facts_stages(net, facts_ref, facts_got, facts_sum):
    net.start(("facts", 0), facts_ref, facts_got.at[0], net.device(c=1 - net.c))

    def pair():
        net.wait(("facts", 0), facts_got.at[0])
        facts_sum[0] = facts_ref[...] + facts_got[0]
        for j in (1, 2, 3):
            there = net.device(z=net.zh * 4 + mod(net.zl + j, 4))
            net.start(("facts", j), facts_sum.at[0], facts_got.at[j], there)

    def near():
        for j in (1, 2, 3):
            net.wait(("facts", j), facts_got.at[j])
        facts_sum[1] = facts_sum[0] + facts_got[1] + facts_got[2] + facts_got[3]
        for j in (1, 2, 3):
            there = net.device(x=mod(net.x + j, 4))
            net.start(("facts", 3 + j), facts_sum.at[1], facts_got.at[3 + j], there)

    def whole():
        for j in (1, 2, 3):
            net.wait(("facts", 3 + j), facts_got.at[3 + j])
        facts_sum[2] = facts_sum[1] + facts_got[4] + facts_got[5] + facts_got[6]

    return pair, near, whole


def gather(net, core, pool_ref, cot_ref, facts_ref, bufs, padded, landed, facts_got, facts_sum):
    partner = net.device(c=1 - net.c)
    here = (net.zh, net.y, net.x, net.zl)
    own_rows = pl.ds(16 * core, 16)
    for o in range(3):
        columns = slice(o * 128, (o + 1) * 128)
        if kind(core, o) == "cot":
            dst = bufs["pool"].at[(o,) + here + (own_rows,)]
            net.start(("swap", o), pool_ref.at[:, pl.ds(o * 128, 128)], dst, partner)
        else:
            block = cot_ref[:, columns].astype(F32)
            padded[o] = jnp.concatenate([block, jnp.zeros((8, 128), F32)], axis=0).astype(BF16)
            net.start(("swap", o), padded.at[o], landed.at[o], partner)
    for o in range(3):
        columns = slice(o * 128, (o + 1) * 128)
        if kind(core, o) == "pool":
            bufs["pool"][(o,) + here + (own_rows,)] = pool_ref[:, columns]
            net.wait(("swap", o), bufs["pool"].at[(o,) + here + (pl.ds(16 * (1 - core), 16),)])
        else:
            net.wait(("swap", o), landed.at[o])
            own = cot_ref[:, columns].astype(F32)
            other = landed[o].astype(F32)[:PROMPT]
            pair = [own, other] if core == 0 else [other, own]
            bufs["cot"][(o,) + here] = jnp.concatenate(pair, axis=0).astype(BF16)
    work = Gather(net, core, bufs)
    work.run(facts_stages(net, facts_ref, facts_got, facts_sum))
    return [(key, copy.src_ref.shape, copy.src_ref.dtype) for key, copy in net.sent.items()]


def build_facts(net, ids_ref, tenant_ref, lengths_ref, routes_ref, route_weight_ref, facts_ref):
    sequence = (net.x * 4 + net.zl) * 2 + net.c
    row = lax.broadcasted_iota(jnp.int32, (PROMPT, TOKENS), 0) + sequence * PROMPT
    place = jnp.where(lax.broadcasted_iota(jnp.int32, (PROMPT, TOKENS), 1) == row, 1.0, 0.0)
    ids = jnp.broadcast_to(ids_ref[pl.ds(tenant_ref[0], 1), :].astype(F32), (8, PROMPT))
    spread = jnp.dot(
        ids, place, precision=lax.Precision.HIGHEST, preferred_element_type=F32
    )
    facts_ref[...] = jnp.zeros_like(facts_ref)
    facts_ref[0:1] = spread[0:1]
    live = place * jnp.where(
        lax.broadcasted_iota(jnp.int32, (PROMPT, TOKENS), 0) < lengths_ref[0], 1.0, 0.0
    )
    facts_ref[1:2] = jnp.sum(live, axis=0, keepdims=True)
    for k in range(2):
        route = routes_ref[:, k : k + 1].astype(F32)
        facts_ref[2 + k : 3 + k] = jnp.sum(place * route, axis=0, keepdims=True)
        weight = route_weight_ref[:, k : k + 1]
        facts_ref[4 + k : 5 + k] = jnp.sum(live * weight, axis=0, keepdims=True)


def kernel(
    pool_ref,
    cot_ref,
    ids_ref,
    tenant_ref,
    lengths_ref,
    routes_ref,
    route_weight_ref,
    gain_ref,
    w_gate_hbm,
    w_up_hbm,
    w_down_hbm,
    out_ref,
    pool_buf,
    cot_buf,
    w_in,
    w_out,
    padded,
    landed,
    facts_got,
    facts_sum,
    hidden,
    back,
    squares,
    scales,
    grads,
    part_out,
    part_in,
    sums,
    first_a,
    first_b,
    mid_a,
    mid_b,
    second_a,
    second_b,
    plane,
    last,
    dot_own,
    dot_pair,
    dot_sum,
    dot_x,
    dot_y,
    dot_z,
    gain_all,
    facts_ref,
    weight_sems,
    send_sems,
    recv_sems,
):
    gain_all[...] = gain_ref[...].astype(F32)
    net = Net(send_sems, recv_sems)
    partner = net.device(c=1 - net.c)
    loads = [
        pltpu.make_async_copy(w_gate_hbm, w_in.at[:, :, pl.ds(0, 128)], weight_sems.at[0]),
        pltpu.make_async_copy(w_up_hbm, w_in.at[:, :, pl.ds(128, 128)], weight_sems.at[1]),
        pltpu.make_async_copy(w_down_hbm, w_out, weight_sems.at[2]),
    ]
    for load in loads:
        load.start()

    build_facts(net, ids_ref, tenant_ref, lengths_ref, routes_ref, route_weight_ref, facts_ref)
    barrier = pltpu.get_barrier_semaphore()
    peers = [partner]
    for j in (1, 2, 3):
        peers += [net.device(x=mod(net.x + j, 4)), net.device(y=mod(net.y + j, 4))]
    peers += [net.device(z=mod(net.z + j, 16)) for j in NEAR]
    for peer in peers:
        pl.semaphore_signal(barrier, inc=1, device_id=peer, device_id_type=MESH)
    pl.semaphore_wait(barrier, len(peers))

    bufs = {"pool": pool_buf, "cot": cot_buf}
    sizes = [None, None]
    for core in range(2):

        @pl.when(net.c == core)
        def _():
            branch = Net(send_sems, recv_sems)
            branch.slots = net.slots
            sizes[core] = gather(
                branch, core, pool_ref, cot_ref, facts_ref, bufs, padded, landed, facts_got, facts_sum
            )

    for load in loads:
        load.wait()

    def stand_in(shape, dtype):
        if dtype == F32:
            return facts_sum.at[0]
        if shape == (16, 128):
            return padded.at[0, pl.ds(0, 16)]
        if shape == (32, 128):
            return padded.at[0]
        buf = pool_buf if shape[-2] == POOL_ROWS else cot_buf
        ref = buf.at[(0,) * (7 - len(shape))]
        assert ref.shape == shape
        return ref

    def drain_gather():
        for core in range(2):

            @pl.when(net.c == core)
            def _():
                net.drain_sizes(sizes[core], stand_in)
                Gather(net, core, bufs).drain()

    hidden[...] = jnp.zeros_like(hidden)
    back[...] = jnp.zeros_like(back)
    squares[...] = jnp.zeros_like(squares)
    for o in range(3):

        def columns_step(zh, carry, o=o):
            blocks = [(zh * 4 + y) * 3 + o for y in range(4)]
            normed = []
            square = None
            for y in range(4):
                value = pool_buf[o, zh, y].reshape(16 * POOL_ROWS, 128).astype(F32)
                square = value * value if square is None else square + value * value
                normed.append((value * gain_all[pl.ds(blocks[y], 1), :]).astype(BF16))
            squares[...] += square
            weights = jnp.concatenate([w_in[b] for b in blocks], axis=0)
            hidden[...] += jnp.dot(
                jnp.concatenate(normed, axis=1), weights, preferred_element_type=F32
            )
            cots = jnp.concatenate(
                [cot_buf[o, zh, y].reshape(TOKENS, 128) for y in range(4)], axis=1
            )
            downs = jnp.concatenate(
                [w_out[:, pl.ds(pl.multiple_of(b * 128, 128), 128)] for b in blocks], axis=1
            )
            back[...] += lax.dot_general(cots, downs, NT, preferred_element_type=F32)
            return carry

        for core in range(2):

            @pl.when(net.c == core)
            def _():
                Gather(net, core, bufs).landed(o)

        lax.fori_loop(0, 4, columns_step, 0)

    ids = facts_sum[2, 0:1]
    live = facts_sum[2, 1:2]
    expert = (net.zl * 2 + net.c).astype(F32)
    weight = jnp.where(facts_sum[2, 2:3] == expert, facts_sum[2, 4:5], 0.0) + jnp.where(
        facts_sum[2, 3:4] == expert, facts_sum[2, 5:6], 0.0
    )
    back_all = back[...]
    back_hi = back_all.astype(BF16)
    back_lo = (back_all - back_hi.astype(F32)).astype(BF16)

    def rows_step(i, carry):
        rows = pl.ds(pl.multiple_of(i * 128, 128), 128)
        number = (lax.broadcasted_iota(jnp.int32, (128, 1), 0) + i * 128).astype(F32)
        place = jnp.where(ids == number, weight, 0.0)
        place_hi = place.astype(BF16)
        place_lo = (place - place_hi.astype(F32)).astype(BF16)
        got = jnp.dot(place_hi, back_hi, preferred_element_type=F32)
        got += jnp.dot(place_hi, back_lo, preferred_element_type=F32)
        got += jnp.dot(place_lo, back_hi, preferred_element_type=F32)
        scale = lax.rsqrt(jnp.sum(squares[rows], axis=1, keepdims=True) / D + EPSILON)
        scales[rows] = jnp.broadcast_to(scale, (128, 128))
        raw_gate, raw_up = hidden[rows, 0:128], hidden[rows, 128:256]
        gate, up = raw_gate * scale, raw_up * scale
        sigma = jax.nn.sigmoid(gate)
        grad_gate = got * up * sigma * (1.0 + gate * (1.0 - sigma))
        grad_up = got * (gate * sigma)
        both = jnp.concatenate([grad_gate, grad_up], axis=1).astype(BF16).reshape(4, 2, 16, 256)
        half = pl.ds(pl.multiple_of(i * 64, 64), 64)
        grads[0, half] = both[:, 0].reshape(64, 256)
        grads[1, half] = both[:, 1].reshape(64, 256)
        product = grad_gate * raw_gate + grad_up * raw_up
        dot_own[:, rows] = lax.dot_general(
            jnp.ones((8, 128), F32),
            product,
            NT,
            precision=lax.Precision.HIGHEST,
            preferred_element_type=F32,
        )
        return carry

    lax.fori_loop(0, 4, rows_step, 0)

    def product(parity, zh, y):
        weights = jnp.concatenate([w_in[(zh * 4 + y) * 3 + o] for o in range(3)], axis=0)
        return lax.dot_general(grads[parity], weights, NT, preferred_element_type=F32)

    net.start("dot_pair", dot_own, dot_pair, partner)
    spots = [mod(net.zh + step, 4) for step in GROUP_ORDER]

    def other(g):
        zh = spots[g]

        def other_step(y, carry):
            part_out[zh, y] = product(1 - net.c, zh, y).astype(BF16).reshape(4, 4, 16, 384)
            return carry

        lax.fori_loop(0, 4, other_step, 0)
        net.start(("part", g), part_out.at[zh], part_in.at[zh], partner)

    lanes = [pl.ds(pl.multiple_of(mod(net.x + j, 4) * 128, 128), 128) for j in range(4)]

    def begin(g):
        zh = spots[g]
        net.wait(("part", g), part_in.at[zh])

        def own_step(y, carry):
            total = product(net.c, zh, y).reshape(4, 4, 16, 384) + part_in[zh, y].astype(F32)
            sums[zh, y] = total.astype(BF16)
            return carry

        lax.fori_loop(0, 4, own_step, 0)
        for h in range(2):
            for j in (2, 1, 3):
                x, y = mod(net.x + j, 4), mod(net.y + j, 4)
                to_x, to_y = net.device(x=x), net.device(y=y)
                net.start(("a1", g, h, j), sums.at[zh, :, x, h], first_a.at[g, h, j - 1], to_x)
                net.start(("b1", g, h, j), sums.at[zh, y, :, 2 + h], first_b.at[g, h, j - 1], to_y)

    def middle(g, h):
        zh = spots[g]
        for j in (1, 2, 3):
            net.wait(("a1", g, h, j), first_a.at[g, h, j - 1])
            net.wait(("b1", g, h, j), first_b.at[g, h, j - 1])
        own_a = sums[zh, :, net.x, h].astype(F32)
        own_b = sums[zh, net.y, :, 2 + h].astype(F32)
        for j in range(3):
            own_a += first_a[g, h, j].astype(F32)
            own_b += first_b[g, h, j].astype(F32)
        mid_a[g, h] = own_a.astype(BF16)
        mid_b[g, h] = own_b.astype(BF16)
        for j in (2, 1, 3):
            x, y = mod(net.x + j, 4), mod(net.y + j, 4)
            to_x, to_y = net.device(x=x), net.device(y=y)
            net.start(("a2", g, h, j), mid_a.at[g, h, y], second_a.at[g, h, j - 1], to_y)
            net.start(("b2", g, h, j), mid_b.at[g, h, x], second_b.at[g, h, j - 1], to_x)

    def line_copy(g, zl):
        slot = GROUP_ORDER[g] * 4 + mod(zl + 4 - net.zl, 4)
        there = net.device(z=spots[g] * 4 + zl)
        return net.copy_at(Slots.Z + slot, plane.at[g, zl], last.at[slot], there)

    def finish(g, h):
        for j in (1, 2, 3):
            net.wait(("a2", g, h, j), second_a.at[g, h, j - 1])
            net.wait(("b2", g, h, j), second_b.at[g, h, j - 1])
        own_a = mid_a[g, h, net.y].astype(F32)
        own_b = mid_b[g, h, net.x].astype(F32)
        for j in range(3):
            own_a += second_a[g, h, j].astype(F32)
            own_b += second_b[g, h, j].astype(F32)
        plane[g, h] = own_a.astype(BF16)
        plane[g, 2 + h] = own_b.astype(BF16)
        for zl in (h, 2 + h):
            if GROUP_ORDER[g] > 0:
                line_copy(g, zl).start()
            else:
                pl.when(net.zl != zl)(lambda zl=zl: line_copy(g, zl).start())

    def dot_one():
        net.wait("dot_pair", dot_pair)
        dot_sum[...] = dot_own[...] + dot_pair[...]
        for j in (1, 2, 3):
            net.start(
                ("dot_x", j), dot_sum.at[:, lanes[j]], dot_x.at[j], net.device(x=mod(net.x + j, 4))
            )

    def dot_two():
        for j in (1, 2, 3):
            net.wait(("dot_x", j), dot_x.at[j])
        dot_y[0] = dot_sum[:, lanes[0]] + dot_x[1] + dot_x[2] + dot_x[3]
        for j in (1, 2, 3):
            net.start(("dot_y", j), dot_y.at[0], dot_y.at[j], net.device(y=mod(net.y + j, 4)))

    def dot_three():
        for j in (1, 2, 3):
            net.wait(("dot_y", j), dot_y.at[j])
        dot_z[0] = dot_y[0] + dot_y[1] + dot_y[2] + dot_y[3]
        for j in range(1, 16):
            net.start(("dot_z", j), dot_z.at[0], dot_z.at[j], net.device(z=mod(net.z + j, 16)))

    other(0)
    other(1)
    begin(0)
    dot_one()
    other(2)
    begin(1)
    dot_two()
    middle(0, 0)
    middle(0, 1)
    other(3)
    begin(2)
    dot_three()
    middle(1, 0)
    finish(0, 0)
    middle(1, 1)
    finish(0, 1)
    begin(3)
    drain_gather()
    middle(2, 0)
    finish(1, 0)
    middle(2, 1)
    finish(1, 1)

    first = ((net.x * 4 + net.zl) * 2 + net.c) * 16
    own_number = (lax.broadcasted_iota(jnp.int32, (16, 1), 0) + first).astype(F32)
    own_place = jnp.where(ids == own_number, live, 0.0).astype(BF16)
    direct = jnp.concatenate(
        [
            jnp.dot(
                own_place,
                cot_buf[o, net.zh, net.y].reshape(TOKENS, 128),
                preferred_element_type=F32,
            )
            for o in range(3)
        ],
        axis=1,
    )

    middle(3, 0)
    finish(2, 0)
    middle(3, 1)
    finish(2, 1)
    finish(3, 0)
    finish(3, 1)
    net.drain()

    for j in range(1, 16):
        net.wait(("dot_z", j), dot_z.at[j])
    dots = dot_z[0]
    for j in range(1, 16):
        dots += dot_z[j]
    own_lane = (net.zl * 2 + net.c) * 16 + lax.broadcasted_iota(jnp.int32, (16, 128), 0)
    picked = jnp.where(lax.broadcasted_iota(jnp.int32, (16, 128), 1) == own_lane, dots[0:1], 0.0)
    own_dot = jnp.sum(picked, axis=1, keepdims=True)
    scale = scales[pl.ds(pl.multiple_of(first, 16), 16), 0:1]
    factor = scale * scale * scale * own_dot / D

    tile = (net.zh * 4 + net.y) * 3
    own_gain = jnp.concatenate([gain_all[pl.ds(tile + o, 1), :] for o in range(3)], axis=1)
    total = plane[3, net.zl].astype(F32)
    for step in GROUP_ORDER:
        for j in range(4):
            slot = step * 4 + j
            if slot > 0:
                arrival = last.at[slot]
                net.copy_at(Slots.Z + slot, arrival, arrival, partner).wait_recv()
                total += last[slot].astype(F32)
    out_ref[...] = (
        direct + scale * own_gain * total - pool_ref[...].astype(F32) * factor
    )
    for slot in range(1, 16):
        net.copy_at(Slots.Z + slot, plane.at[0, 0], last.at[slot], partner).wait_send()


def local(
    pool,
    prompt_ids,
    tenant,
    lengths,
    routes,
    route_weight,
    cotangent,
    norm_gain,
    w_gate,
    w_up,
    w_down,
):
    gain = norm_gain.reshape(48, 128)
    vmem = pl.BlockSpec(memory_space=pltpu.VMEM)
    hbm = pl.BlockSpec(memory_space=pl.ANY)
    smem = pl.BlockSpec(memory_space=pltpu.SMEM)
    sums_shape = pltpu.VMEM((4, 4, 4, 4, 16, 384), BF16)
    copies = Slots.COUNT
    return pl.pallas_call(
        kernel,
        out_shape=jax.ShapeDtypeStruct((16, 384), F32),
        in_specs=[vmem] * 3 + [smem] * 2 + [vmem] * 3 + [hbm] * 3,
        out_specs=vmem,
        scratch_shapes=[
            pltpu.VMEM((3, 4, 4, 4, 4, POOL_ROWS, 128), BF16),
            pltpu.VMEM((3, 4, 4, 4, 4, COT_ROWS, 128), BF16),
            pltpu.VMEM((48, 128, 256), BF16),
            pltpu.VMEM((128, D), BF16),
            pltpu.VMEM((3, 32, 128), BF16),
            pltpu.VMEM((3, 32, 128), BF16),
            pltpu.VMEM((7, 8, TOKENS), F32),
            pltpu.VMEM((3, 8, TOKENS), F32),
            pltpu.VMEM((512, 256), F32),
            pltpu.VMEM((TOKENS, 128), F32),
            pltpu.VMEM((512, 128), F32),
            pltpu.VMEM((512, 128), F32),
            pltpu.VMEM((2, 256, 256), BF16),
            sums_shape,
            sums_shape,
            sums_shape,
            pltpu.VMEM((4, 2, 3, 4, 16, 384), BF16),
            pltpu.VMEM((4, 2, 3, 4, 16, 384), BF16),
            pltpu.VMEM((4, 2, 4, 16, 384), BF16),
            pltpu.VMEM((4, 2, 4, 16, 384), BF16),
            pltpu.VMEM((4, 2, 3, 16, 384), BF16),
            pltpu.VMEM((4, 2, 3, 16, 384), BF16),
            pltpu.VMEM((4, 4, 16, 384), BF16),
            pltpu.VMEM((16, 16, 384), BF16),
            pltpu.VMEM((8, 512), F32),
            pltpu.VMEM((8, 512), F32),
            pltpu.VMEM((8, 512), F32),
            pltpu.VMEM((4, 8, 128), F32),
            pltpu.VMEM((4, 8, 128), F32),
            pltpu.VMEM((16, 8, 128), F32),
            pltpu.VMEM((48, 128), F32),
            pltpu.VMEM((8, TOKENS), F32),
            pltpu.SemaphoreType.DMA((3,)),
            pltpu.SemaphoreType.DMA((copies,)),
            pltpu.SemaphoreType.DMA((copies,)),
        ],
        compiler_params=pltpu.CompilerParams(
            collective_id=0, has_side_effects=True, vmem_limit_bytes=56 * 2**20
        ),
        name="moe_backward",
    )(
        pool,
        cotangent,
        prompt_ids,
        tenant,
        lengths,
        routes,
        route_weight,
        gain,
        w_gate.reshape(48, 128, 128),
        w_up.reshape(48, 128, 128),
        w_down[0],
    )


def solution(mesh):
    placed = (
        P(("dp", "expert"), "tensor"),
        P(),
        P(("dp", "expert")),
        P(("dp", "expert")),
        P(("dp", "expert"), None),
        P(("dp", "expert"), None),
        P(("dp", "expert"), "tensor"),
        P(),
        P("expert", None, ("dp", "tensor")),
        P("expert", None, ("dp", "tensor")),
        P("expert", ("dp", "tensor"), None),
    )
    return jax.shard_map(
        local, mesh=mesh, in_specs=placed, out_specs=P(("dp", "expert"), "tensor"), check_vma=False
    )
```
